256 devices in a mesh: blk: 64 (over x, y, z_hi, core), uly: 4 (over z_lo).
Axes of the slice: x: 4, y: 4, z: 8 (z_hi: 2, z_lo: 4; z = z_hi * 4 + z_lo), core: 2. Of those that a mesh axis runs over, the one named last changes fastest.
Arguments:
- queries: bfloat16 [16384, 512], P(('blk', 'uly')), may hold values from -10 to 10
- key_vectors: bfloat16 [16384, 512], P(('blk', 'uly')), may hold values from -10 to 10
- value_vectors: bfloat16 [16384, 512], P(('blk', 'uly')), may hold values from -16 to 16
- tangent_queries: bfloat16 [16384, 512], P(('blk', 'uly')), may hold values from -6 to 6
- tangent_keys: bfloat16 [16384, 512], P(('blk', 'uly')), may hold values from -6 to 6
- tangent_values: bfloat16 [16384, 512], P(('blk', 'uly')), may hold values from -6 to 6
- positions: int32 [3, 16384], P(None, ('blk', 'uly')), may hold values from 0 to 51, as said below
- out_weight: bfloat16 [512, 5120], P('uly', 'blk'), may hold values from -0.25 to 0.25
Outputs:
- attention_out: bfloat16 [16384, 5120], P(('blk', 'uly'))
- tangent_out: bfloat16 [16384, 5120], P(('blk', 'uly'))
The draws below stay inside these ranges and needn't reach their ends.
Inputs may be any that keep to these rules, and one draw needn't show every extreme that they name: `positions`: token n lies at raster index s + n of a latent grid of frames of 30 rows and 52 columns, for one offset s of each draw: frame (s + n) // 1560, row ((s + n) // 52) % 30, column (s + n) % 52.
All inputs are finite; a program needn't handle non-finite values.
Results may differ from the reference program's by a relative error of at most 0.017.
Values may be sent and summed in bfloat16 or wider, within the bound.
A program may use at most 64 MiB of HBM per device.

```python
import math
import jax
import jax.numpy as jnp
from jax import lax

D = 5120
HEADS = 4
HEAD_DIM = 128
INNER = 512
SEQ = 16384


def draw_queries(key, part):
    key = jax.random.fold_in(key, 11)
    result = jnp.clip(1.6 * jax.random.normal(key, (SEQ, INNER), jnp.float32), -8.0, 8.0)
    return result.astype(jnp.bfloat16)


def draw_key_vectors(key, part):
    key = jax.random.fold_in(key, 13)
    result = jnp.clip(1.6 * jax.random.normal(key, (SEQ, INNER), jnp.float32), -8.0, 8.0)
    return result.astype(jnp.bfloat16)


def draw_positions(key, part):
    key = jax.random.fold_in(key, 17)
    span = max(32760 - SEQ, 1)
    start = jax.random.randint(key, (), 0, span).astype(jnp.int32)
    index = jnp.arange(SEQ).astype(jnp.int32) + start
    frame_ids = index // 1560
    row_ids = index // 52 % 30
    column_ids = index % 52
    return jnp.stack([frame_ids, row_ids, column_ids]).astype(jnp.int32)


def block_scale(own_key, dims, cuts, low, high):
    gain, own = 1.0, jax.random.fold_in(own_key, 6)
    for position, shards_of in cuts:
        heights = jnp.exp(jax.random.uniform(jax.random.fold_in(own, position), (shards_of,), jnp.float32, low / len(cuts), high / len(cuts)))
        gain = gain * jnp.repeat(heights, dims[position] // shards_of).reshape([-1 if axis == position else 1 for axis in range(len(dims))])
    return gain


def noise(key, shape, deviation, limit, pieces=(), kind=jnp.bfloat16):
    values = deviation * jax.random.normal(key, shape, jnp.float32)
    if pieces:
        values = values * block_scale(key, shape, pieces, -0.22, 0.18)
    return jnp.clip(values, -limit, limit).astype(kind)


def setup_inputs(seed: int = 0) -> dict:
    keys = jax.random.split(jax.random.key(seed), 9)
    queries = draw_queries(jax.random.fold_in(keys[8], 71), 0)
    key_vectors = draw_key_vectors(jax.random.fold_in(keys[8], 71), 0)
    value_vectors = noise(keys[2], (SEQ, INNER), 3.0, 16.0, ((0, 256),))
    tangent_queries = noise(keys[3], (SEQ, INNER), 1.0, 6.0, ((0, 256),))
    tangent_keys = noise(keys[4], (SEQ, INNER), 1.0, 6.0, ((0, 256),))
    tangent_values = noise(keys[5], (SEQ, INNER), 1.0, 6.0, ((0, 256),))
    positions = draw_positions(jax.random.fold_in(keys[8], 71), 0)
    out_weight = noise(keys[7], (INNER, D), INNER ** -0.5, 0.25, ((0, 4), (1, 64)))
    return dict(queries=queries, key_vectors=key_vectors, value_vectors=value_vectors, tangent_queries=tangent_queries, tangent_keys=tangent_keys, tangent_values=tangent_values, positions=positions, out_weight=out_weight)


score_scale = 0.08838834764831845


def rope_angles(positions):
    pair_index = jnp.arange(64)
    section_begin = jnp.where(pair_index >= 43, 43, jnp.where(pair_index >= 22, 22, 0))
    section_length = jnp.where(pair_index >= 22, 21.0, 22.0).astype(jnp.float32)
    frequency = jnp.power(jnp.float32(10000.0), -(pair_index - section_begin).astype(jnp.float32) / section_length)
    frames = positions[0][:, None]
    rows_pos = positions[1][:, None]
    columns = positions[2][:, None]
    chosen = jnp.where(pair_index[None, :] < 22, frames, jnp.where(pair_index[None, :] < 43, rows_pos, columns))
    angle = chosen.astype(jnp.float32) * frequency[None, :]
    return jnp.cos(angle), jnp.sin(angle)


def rotate(vectors, cosine, sine_table):
    count = vectors.shape[0]
    split = vectors.reshape(count, -1, 128).astype(jnp.float32)
    first_half = split[..., :64]
    second_half = split[..., 64:]
    cos_part = cosine[:, None, :]
    sin_part = sine_table[:, None, :]
    turned = jnp.concatenate([first_half * cos_part - second_half * sin_part, second_half * cos_part + first_half * sin_part], axis=-1)
    return turned.reshape(count, -1).astype(jnp.bfloat16)


def attend_head(query, key_rows, value_rows, tan_query, tan_key, tan_value):
    scores = jnp.dot(query, key_rows.T, preferred_element_type=jnp.float32) * score_scale
    tan_scores = (jnp.dot(tan_query, key_rows.T, preferred_element_type=jnp.float32) + jnp.dot(query, tan_key.T, preferred_element_type=jnp.float32)) * score_scale
    row_max = jnp.max(scores, axis=1, keepdims=True)
    weights = jnp.exp(scores - row_max)
    weighted = weights * tan_scores
    total = jnp.sum(weights, axis=1)
    slope = jnp.sum(weighted, axis=1)
    weights_low = weights.astype(jnp.bfloat16)
    weighted_low = weighted.astype(jnp.bfloat16)
    first = jnp.dot(weights_low, value_rows, preferred_element_type=jnp.float32)
    second = jnp.dot(weighted_low, value_rows, preferred_element_type=jnp.float32) + jnp.dot(weights_low, tan_value, preferred_element_type=jnp.float32)
    output = first / total[:, None]
    tangent = second / total[:, None] - (slope / total)[:, None] * output
    return output.astype(jnp.bfloat16), tangent.astype(jnp.bfloat16)


def reference(queries, key_vectors, value_vectors, tangent_queries, tangent_keys, tangent_values, positions, out_weight):
    cosine, sine_table = rope_angles(positions)
    rot_query = rotate(queries, cosine, sine_table)
    rot_key = rotate(key_vectors, cosine, sine_table)
    rot_tquery = rotate(tangent_queries, cosine, sine_table)
    rot_tkey = rotate(tangent_keys, cosine, sine_table)
    block_rows = math.gcd(SEQ, 512)

    def per_head(head_index):
        offset = (head_index * HEAD_DIM).astype(jnp.int32)

        def cut(array):
            return lax.dynamic_slice_in_dim(array, offset, HEAD_DIM, 1)

        head_query, head_key, head_value, head_tquery, head_tkey, head_tvalue = [cut(a) for a in (rot_query, rot_key, value_vectors, rot_tquery, rot_tkey, tangent_values)]

        def per_block(block_index):
            start = (block_index * block_rows).astype(jnp.int32)
            query_rows = lax.dynamic_slice_in_dim(head_query, start, block_rows, 0)
            tquery_rows = lax.dynamic_slice_in_dim(head_tquery, start, block_rows, 0)
            return attend_head(query_rows, head_key, head_value, tquery_rows, head_tkey, head_tvalue)

        outputs, tangents = lax.map(per_block, jnp.arange(SEQ // block_rows).astype(jnp.int32))
        return outputs.reshape(SEQ, HEAD_DIM), tangents.reshape(SEQ, HEAD_DIM)

    mixed_heads, dmixed_heads = lax.map(per_head, jnp.arange(HEADS).astype(jnp.int32))
    mixed = mixed_heads.transpose(1, 0, 2).reshape(SEQ, INNER)
    dmixed = dmixed_heads.transpose(1, 0, 2).reshape(SEQ, INNER)
    attention_out = jnp.dot(mixed, out_weight, preferred_element_type=jnp.float32).astype(jnp.bfloat16)
    tangent_out = jnp.dot(dmixed, out_weight, preferred_element_type=jnp.float32).astype(jnp.bfloat16)
    return attention_out, tangent_out
```

```python
import functools

import jax
import jax.numpy as jnp
from jax import lax
from jax.experimental import pallas as pl
from jax.experimental.pallas import tpu as pltpu
from jax.sharding import PartitionSpec as P

MESH = pl.DeviceIdType.MESH
SCALE = 0.08838834764831845
SCALE2 = SCALE * 1.4426950408889634
NT = (((1,), (1,)), ((), ()))
NN = (((1,), (0,)), ((), ()))

X, Y, Z = 4, 4, 8
ROWS = 64
BLOCK = X * ROWS
PIECES = 7


def dot(a, b, dims):
    return lax.dot_general(a, b, dims, preferred_element_type=jnp.float32)


def place():
    blk, zlo = lax.axis_index("blk"), lax.axis_index("uly")
    return blk // 16, lax.rem(blk // 4, 4), lax.rem(blk // 2, 2) * 4 + zlo, lax.rem(blk, 2)


def device(x, y, z, core):
    return (((x * 4 + y) * 2 + z // 4) * 2 + core, lax.rem(z, 4))


def rotary_tables(pos_ref):
    lane = lax.broadcasted_iota(jnp.int32, (128, 128), 0)
    pair = jnp.where(lane >= 64, lane - 64, lane)
    begin = jnp.where(pair >= 43, 43, jnp.where(pair >= 22, 22, 0))
    length = jnp.where(pair >= 22, 21.0, 22.0)
    frequency = jnp.exp((pair - begin).astype(jnp.float32) / length * -9.210340371976184)
    pos = pos_ref[...].astype(jnp.float32)
    pos = jnp.concatenate([pos, pos], axis=1)
    chosen = jnp.where(pair < 22, pos[0:1], jnp.where(pair < 43, pos[1:2], pos[2:3]))
    angle = chosen * frequency
    cosine = jnp.cos(angle)
    sine = jnp.where(lane < 64, -jnp.sin(angle), jnp.sin(angle))
    return cosine.T[:ROWS], sine.T[:ROWS]


def fold(keys, q_ref, acc1, acc2, top, total, slope, rows):
    q = q_ref[rows, :]
    s = dot(q[:, 128:], keys[:, :128], NT)
    t = dot(q, keys[:, :256], NT)
    lanes = [slice(i * 128, (i + 1) * 128) for i in range(keys.shape[0] // 128)]
    high = functools.reduce(jnp.maximum, [s[:, i] for i in lanes])
    old = top[rows, :]
    new = jnp.maximum(old, jnp.max(high, axis=1, keepdims=True) * SCALE2)
    shrink = jnp.exp2(old - new)
    weights = [jnp.exp2(s[:, i] * SCALE2 - new) for i in lanes]
    tilted = [w * t[:, i] for w, i in zip(weights, lanes)]
    top[rows, :] = new
    total[rows, :] = total[rows, :] * shrink + functools.reduce(jnp.add, weights)
    slope[rows, :] = slope[rows, :] * shrink + functools.reduce(jnp.add, tilted)
    low = jnp.concatenate([w.astype(jnp.bfloat16) for w in weights], axis=1)
    tilted = jnp.concatenate([w.astype(jnp.bfloat16) for w in tilted], axis=1)
    both = jnp.concatenate([shrink, shrink], axis=1)
    acc1[rows, :] = acc1[rows, :] * both + dot(low, keys[:, 256:], NN)
    acc2[rows, :] = acc2[rows, :] * shrink + dot(tilted, keys[:, 256:384], NN)


def kernel(
    q_ref, k_ref, v_ref, tq_ref, tk_ref, tv_ref, pos_ref, w_ref, out_ref, tout_ref,
    kv_send, q_send, kv, qs, wbuf, wsquare, acc1, acc2, top, total, slope,
    part_send, stat_send, part, stat, mix, heads,
    s_akv, r_akv, s_aq, r_aq, s_ring, r_ring, s_twin, r_twin, s_yq, r_yq,
    s_wz, r_wz, s_w1, r_w1, s_w2, r_w2, s_w3, r_w3, s_part, r_part, s_stat, r_stat, s_ret, r_ret,
):
    x, y, z, core = place()
    along_x = [device(lax.rem(x + d, X), y, z, core) for d in range(X)]
    along_y = [device(x, lax.rem(y + d, Y), z, core) for d in range(Y)]
    along_z = [device(x, y, lax.rem(z + d, Z), core) for d in range(Z)]
    twin = device(x, y, z, 1 - core)

    barrier = pltpu.get_barrier_semaphore()
    partners = along_x[1:] + along_y[1:] + along_z[1:] + [twin]
    for partner in partners:
        pl.semaphore_signal(barrier, inc=1, device_id=partner, device_id_type=MESH)

    sends = []

    def send(src, dst, s, r, target):
        copy = pltpu.make_async_remote_copy(
            src_ref=src, dst_ref=dst, send_sem=s, recv_sem=r, device_id=target, device_id_type=MESH
        )
        copy.start()
        sends.append(copy)
        return copy

    cosine, sine = rotary_tables(pos_ref)

    def rotated(ref, h):
        a = ref[:, h * 128 : (h + 1) * 128].astype(jnp.float32)
        return (a * cosine + pltpu.roll(a, 64, 1) * sine).astype(jnp.bfloat16)

    for h in range(X):
        cut = slice(h * 128, (h + 1) * 128)
        q_send[h, :, :128] = rotated(tq_ref, h)
        q_send[h, :, 128:] = rotated(q_ref, h)
        kv_send[h, :, :128] = rotated(k_ref, h)
        kv_send[h, :, 128:256] = rotated(tk_ref, h)
        kv_send[h, :, 256:384] = v_ref[:, cut]
        kv_send[h, :, 384:] = tv_ref[:, cut]

    wsquare[...] = jnp.zeros_like(wsquare)
    wsquare[:, :80] = w_ref[...].astype(jnp.float32)
    piece = wsquare[...].T[:80].astype(jnp.bfloat16)
    zhi, zlo = z // 4, lax.rem(z, 4)
    own_lanes = pl.ds(pl.multiple_of(zlo * 128, 128), 128)
    own_piece = wbuf.at[x, y * 2 + zhi, core, :, own_lanes]
    own_piece[...] = piece

    pl.semaphore_wait(barrier, len(partners))

    copies_q = []
    for d in range(1, X):
        h = lax.rem(x + d, X)
        e = X - d
        copies_q.append(
            send(q_send.at[h], qs.at[0, pl.ds(e * ROWS, ROWS)], s_aq.at[d], r_aq.at[d], along_x[d])
        )
    copies_kv = []
    for d in range(1, X):
        h = lax.rem(x + d, X)
        e = X - d
        dst = kv.at[0, e // 2, core, pl.ds((e % 2) * ROWS, ROWS)]
        copies_kv.append(send(kv_send.at[h], dst, s_akv.at[d], r_akv.at[d], along_x[d]))
    copies_w = []
    for d in range(1, Z):
        copies_w.append(send(own_piece, own_piece, s_wz.at[d], r_wz.at[d], along_z[d]))
    qs[0, :ROWS] = q_send[x]
    kv[0, 0, core, :ROWS] = kv_send[x]

    top[...] = jnp.full_like(top, -1e30)
    for ref in (acc1, acc2, total, slope):
        ref[...] = jnp.zeros_like(ref)

    for copy in copies_q:
        copy.wait_recv()
    copies_q = [
        send(qs.at[0], qs.at[Y - d], s_yq.at[d], r_yq.at[d], along_y[d]) for d in (1, 3, 2)
    ]
    for copy in copies_kv:
        copy.wait_recv()

    def ring(r, p, src):
        return pltpu.make_async_remote_copy(
            src_ref=src,
            dst_ref=kv.at[p + 1, r, core],
            send_sem=s_ring.at[r, p],
            recv_sem=r_ring.at[r, p],
            device_id=along_z[1] if r == 0 else along_z[Z - 1],
            device_id_type=MESH,
        )

    def across(slot, r):
        here = kv.at[slot, r, core]
        return pltpu.make_async_remote_copy(
            src_ref=here,
            dst_ref=here,
            send_sem=s_twin.at[slot, r],
            recv_sem=r_twin.at[slot, r],
            device_id=twin,
            device_id_type=MESH,
        )

    for p in range(2):
        ring(0, p, kv.at[0, p, core]).start()
        ring(1, p, kv.at[0, 1 - p, core]).start()
    for r in range(2):
        across(0, r).start()

    for copy in copies_w:
        copy.wait_recv()
    own_y = pl.ds(y * 2, 2)
    half_a, half_b = pl.ds(0, 256), pl.ds(256, 256)
    copies_w = []
    for d in (1, 3, 2):
        here = wbuf.at[x, own_y, core, :, half_a]
        copies_w.append(send(here, here, s_w1.at[0, d], r_w1.at[0, d], along_y[d]))
        here = wbuf.at[x, own_y, core, :, half_b]
        copies_w.append(send(here, here, s_w1.at[1, d], r_w1.at[1, d], along_x[d]))

    for copy in copies_q:
        copy.wait_recv()

    def step(j):
        for r in range(2):
            ring(r, j, kv.at[j + 1, r, core]).wait_recv()

            @pl.when(j <= PIECES - 3)
            def _():
                ring(r, j + 2, kv.at[j + 1, r, core]).start()

            across(j + 1, r).start()

    def compute(j):
        for r in range(2):
            across(j, r).wait_recv()
        keys = kv[j].reshape(512, 512)
        fold(keys, qs_rows, acc1, acc2, top, total, slope, pl.ds(0, Y * BLOCK))

    qs_rows = qs.reshape(Y * BLOCK, 256)

    def body(j, carry):
        step(j)
        compute(j)
        return carry

    lax.fori_loop(0, 2, body, 0)

    for copy in copies_w:
        copy.wait_recv()
    copies_w = []
    for d in (1, 3, 2):
        here = wbuf.at[x, :, core, :, half_a]
        copies_w.append(send(here, here, s_w2.at[0, d], r_w2.at[0, d], along_x[d]))
        here = wbuf.at[:, own_y, core, :, half_b]
        copies_w.append(send(here, here, s_w2.at[1, d], r_w2.at[1, d], along_y[d]))

    lax.fori_loop(2, PIECES, body, 0)
    compute(PIECES)

    lane = lax.broadcasted_iota(jnp.int32, (BLOCK, 128), 1)

    def sums(d):
        rows = pl.ds(d * BLOCK, BLOCK)
        first = acc1[rows, :128]
        second = acc1[rows, 128:] + acc2[rows, :] * SCALE
        all_total = jnp.sum(total[rows, :], axis=1, keepdims=True)
        all_slope = jnp.sum(slope[rows, :], axis=1, keepdims=True) * SCALE
        return first, second, top[rows, :], all_total, all_slope

    copies_part = []
    for d in (2, 1, 3):
        first, second, high, all_total, all_slope = sums(d)
        part_send[d - 1, :, :128] = first.astype(jnp.bfloat16)
        part_send[d - 1, :, 128:] = second.astype(jnp.bfloat16)
        packed = jnp.where(lane == 0, high, jnp.where(lane == 1, all_total, all_slope))
        stat_send[d - 1] = packed.T[:8]
        e = Y - d
        copies_part.append(
            send(part_send.at[d - 1], part.at[e - 1], s_part.at[d], r_part.at[d], along_y[d])
        )
        copies_part.append(
            send(stat_send.at[d - 1], stat.at[e - 1], s_stat.at[d], r_stat.at[d], along_y[d])
        )
    for copy in copies_w:
        copy.wait_recv()
    here = wbuf.at[:, :, core]
    copy_w = send(here, here, s_w3.at[0], r_w3.at[0], twin)

    first, second, high, all_total, all_slope = sums(0)
    high = high[:, :1]
    for copy in copies_part:
        copy.wait_recv()
    stats = [
        jnp.concatenate([stat[e], jnp.zeros((120, BLOCK), jnp.float32)], axis=0).T
        for e in range(Y - 1)
    ]
    highest = functools.reduce(jnp.maximum, [a[:, 0:1] for a in stats], high)
    gain = jnp.exp2(high - highest)
    first, second = first * gain, second * gain
    all_total, all_slope = all_total * gain, all_slope * gain
    for e in range(Y - 1):
        gain = jnp.exp2(stats[e][:, 0:1] - highest)
        first = first + part[e, :, :128].astype(jnp.float32) * gain
        second = second + part[e, :, 128:].astype(jnp.float32) * gain
        all_total = all_total + stats[e][:, 1:2] * gain
        all_slope = all_slope + stats[e][:, 2:3] * gain
    inverse = 1.0 / all_total
    mixed = first * inverse
    dmixed = second * inverse - (all_slope * inverse) * mixed
    mix[0] = mixed.astype(jnp.bfloat16)
    mix[1] = dmixed.astype(jnp.bfloat16)

    copies_ret = []
    for d in (2, 1, 3):
        src = mix.at[:, pl.ds(d * ROWS, ROWS)]
        copies_ret.append(send(src, heads.at[x], s_ret.at[d], r_ret.at[d], along_x[d]))
    heads[x] = mix[:, :ROWS]
    copy_w.wait_recv()
    for copy in copies_ret:
        copy.wait_recv()
    lhs = jnp.concatenate([heads[h].reshape(2 * ROWS, 128) for h in range(X)], axis=1)
    width = w_columns = 1280
    for i in range(X):
        weight = wbuf[i].reshape(w_columns, 512)
        result = dot(lhs, weight, NT).astype(jnp.bfloat16)
        out_ref[:, i * width : (i + 1) * width] = result[:ROWS]
        tout_ref[:, i * width : (i + 1) * width] = result[ROWS:]

    for copy in sends:
        copy.wait_send()
    for r in range(2):
        for p in range(PIECES):
            ring(r, p, kv.at[0, 0, core]).wait_send()
        for slot in range(PIECES + 1):
            across(slot, r).wait_send()


def local(*args):
    bf, f32, vmem, dma = jnp.bfloat16, jnp.float32, pltpu.VMEM, pltpu.SemaphoreType.DMA
    pairs = [
        (X,), (X,), (2, PIECES), (PIECES + 1, 2), (Y,), (Z,), (2, X), (2, X), (1,), (Y,), (Y,), (X,),
    ]
    return pl.pallas_call(
        kernel,
        out_shape=[jax.ShapeDtypeStruct((ROWS, 5120), bf)] * 2,
        in_specs=[pl.BlockSpec(memory_space=pltpu.VMEM)] * 8,
        out_specs=[pl.BlockSpec(memory_space=pltpu.VMEM)] * 2,
        scratch_shapes=[
            vmem((X, ROWS, 512), bf),
            vmem((X, ROWS, 256), bf),
            vmem((PIECES + 1, 2, 2, BLOCK // 2, 512), bf),
            vmem((Y, BLOCK, 256), bf),
            vmem((X, 2 * Y, 2, 80, 512), bf),
            vmem((128, 128), f32),
            vmem((Y * BLOCK, 256), f32),
            vmem((Y * BLOCK, 128), f32),
            vmem((Y * BLOCK, 128), f32),
            vmem((Y * BLOCK, 128), f32),
            vmem((Y * BLOCK, 128), f32),
            vmem((Y - 1, BLOCK, 256), bf),
            vmem((Y - 1, 8, BLOCK), f32),
            vmem((Y - 1, BLOCK, 256), bf),
            vmem((Y - 1, 8, BLOCK), f32),
            vmem((2, BLOCK, 128), bf),
            vmem((X, 2, ROWS, 128), bf),
        ]
        + [dma(shape) for shape in pairs for _ in range(2)],
        compiler_params=pltpu.CompilerParams(
            collective_id=0, has_side_effects=True, vmem_limit_bytes=48 << 20
        ),
        name="attend",
    )(*args)


def solution(mesh):
    return jax.shard_map(
        local,
        mesh=mesh,
        in_specs=(
            P(("blk", "uly"), None),
            P(("blk", "uly"), None),
            P(("blk", "uly"), None),
            P(("blk", "uly"), None),
            P(("blk", "uly"), None),
            P(("blk", "uly"), None),
            P(None, ("blk", "uly")),
            P("uly", "blk"),
        ),
        out_specs=(P(("blk", "uly"), None), P(("blk", "uly"), None)),
        check_vma=False,
    )
```

```python
import functools

import jax
import jax.numpy as jnp
from jax import lax
from jax.experimental import pallas as pl
from jax.experimental.pallas import tpu as pltpu
from jax.sharding import PartitionSpec as P

MESH = pl.DeviceIdType.MESH
SCALE = 0.08838834764831845
SCALE2 = SCALE * 1.4426950408889634
NT = (((1,), (1,)), ((), ()))
NN = (((1,), (0,)), ((), ()))

X, Y, Z = 4, 4, 8
ROWS = 64
BLOCK = X * ROWS
PIECES = 14


def dot(a, b, dims):
    return lax.dot_general(a, b, dims, preferred_element_type=jnp.float32)


def place():
    blk, zlo = lax.axis_index("blk"), lax.axis_index("uly")
    return blk // 16, lax.rem(blk // 4, 4), lax.rem(blk // 2, 2) * 4 + zlo, lax.rem(blk, 2)


def device(x, y, z, core):
    return (((x * 4 + y) * 2 + z // 4) * 2 + core, lax.rem(z, 4))


def rotary_tables(pos_ref):
    pair = lax.broadcasted_iota(jnp.int32, (64, 128), 0)
    begin = jnp.where(pair >= 43, 43, jnp.where(pair >= 22, 22, 0))
    length = jnp.where(pair >= 22, 21.0, 22.0)
    frequency = jnp.exp((pair - begin).astype(jnp.float32) / length * -9.210340371976184)
    pos = pos_ref[...].astype(jnp.float32)
    pos = jnp.concatenate([pos, pos], axis=1)
    chosen = jnp.where(pair < 22, pos[0:1], jnp.where(pair < 43, pos[1:2], pos[2:3]))
    angle = chosen * frequency
    cosine, sine = jnp.cos(angle), jnp.sin(angle)
    cosine = jnp.concatenate([cosine, cosine], axis=0)
    sine = jnp.concatenate([-sine, sine], axis=0)
    return cosine.T[:ROWS], sine.T[:ROWS]


def fold(keys, q_ref, acc1, acc2, top, total, slope, rows):
    q = q_ref[rows, :]
    s = dot(q[:, 128:], keys[:, :128], NT)
    t = dot(q, keys[:, :256], NT)
    lanes = [slice(i * 128, (i + 1) * 128) for i in range(keys.shape[0] // 128)]
    high = functools.reduce(jnp.maximum, [s[:, i] for i in lanes])
    old = top[rows, :]
    new = jnp.maximum(old, jnp.max(high, axis=1, keepdims=True) * SCALE2)
    shrink = jnp.exp2(old - new)
    weights = [jnp.exp2(s[:, i] * SCALE2 - new) for i in lanes]
    tilted = [w * t[:, i] for w, i in zip(weights, lanes)]
    top[rows, :] = new
    total[rows, :] = total[rows, :] * shrink + functools.reduce(jnp.add, weights)
    slope[rows, :] = slope[rows, :] * shrink + functools.reduce(jnp.add, tilted)
    low = jnp.concatenate([w.astype(jnp.bfloat16) for w in weights], axis=1)
    tilted = jnp.concatenate([w.astype(jnp.bfloat16) for w in tilted], axis=1)
    both = jnp.concatenate([shrink, shrink], axis=1)
    acc1[rows, :] = acc1[rows, :] * both + dot(low, keys[:, 256:], NN)
    acc2[rows, :] = acc2[rows, :] * shrink + dot(tilted, keys[:, 256:384], NN)


def kernel(
    q_hbm, k_hbm, v_hbm, tq_hbm, tk_hbm, tv_hbm, pos_hbm, w_hbm, heads_hbm, wout_hbm,
    q_ref, k_ref, v_ref, tq_ref, tk_ref, tv_ref, pos_ref,
    kv_send, q_send, kv, qs, wbuf, acc1, acc2, top, total, slope,
    part_send, stat_send, part, stat, mix,
    s_in, s_out, s_akv, r_akv, s_aq, r_aq, s_ring, r_ring, s_twin, r_twin, s_own, r_own, s_yq, r_yq,
    s_wz, r_wz, s_w1, r_w1, s_w2, r_w2, s_w3, r_w3, s_part, r_part, s_stat, r_stat, s_ret, r_ret,
):
    x, y, z, core = place()
    along_x = [device(lax.rem(x + d, X), y, z, core) for d in range(X)]
    along_y = [device(x, lax.rem(y + d, Y), z, core) for d in range(Y)]
    along_z = [device(x, y, lax.rem(z + d, Z), core) for d in range(Z)]
    twin = device(x, y, z, 1 - core)

    zhi, zlo = z // 4, lax.rem(z, 4)
    own_lanes = pl.ds(pl.multiple_of(zlo * 128, 128), 128)
    own_piece = wbuf.at[x, y * 2 + zhi, core, :, own_lanes]
    inputs = [
        (pos_hbm, pos_ref), (tq_hbm, tq_ref), (q_hbm, q_ref), (k_hbm, k_ref), (tk_hbm, tk_ref),
        (v_hbm, v_ref), (tv_hbm, tv_ref), (w_hbm, own_piece),
    ]
    inputs = [pltpu.make_async_copy(a, b, s_in.at[i]) for i, (a, b) in enumerate(inputs)]
    for copy in inputs:
        copy.start()

    barrier = pltpu.get_barrier_semaphore()
    partners = along_x[1:] + along_y[1:] + along_z[1:] + [twin]
    for partner in partners:
        pl.semaphore_signal(barrier, inc=1, device_id=partner, device_id_type=MESH)

    sends = []

    def remote(src, dst, s, r, target):
        return pltpu.make_async_remote_copy(
            src_ref=src, dst_ref=dst, send_sem=s, recv_sem=r, device_id=target, device_id_type=MESH
        )

    def send(*args):
        copy = remote(*args)
        copy.start()
        sends.append(copy)
        return copy

    inputs[0].wait()
    cosine, sine = rotary_tables(pos_ref)

    def rotated(ref, h):
        a = ref[:, h * 128 : (h + 1) * 128].astype(jnp.float32)
        return (a * cosine + pltpu.roll(a, 64, 1) * sine).astype(jnp.bfloat16)

    inputs[7].wait()
    pl.semaphore_wait(barrier, len(partners))
    copies_w = []
    for d in (4, 3, 5, 2, 6, 1, 7):
        copies_w.append(send(own_piece, own_piece, s_wz.at[d], r_wz.at[d], along_z[d]))
    for copy in inputs[1:3]:
        copy.wait()
    for h in range(X):
        q_send[h, :, :128] = rotated(tq_ref, h)
        q_send[h, :, 128:] = rotated(q_ref, h)
    copies_q = []
    for d in (2, 1, 3):
        h = lax.rem(x + d, X)
        e = X - d
        copies_q.append(
            send(q_send.at[h], qs.at[0, pl.ds(e * ROWS, ROWS)], s_aq.at[d], r_aq.at[d], along_x[d])
        )
    for copy in inputs[3:7]:
        copy.wait()
    for h in range(X):
        cut = slice(h * 128, (h + 1) * 128)
        kv_send[h, :, :128] = rotated(k_ref, h)
        kv_send[h, :, 128:256] = rotated(tk_ref, h)
        kv_send[h, :, 256:384] = v_ref[:, cut]
        kv_send[h, :, 384:] = tv_ref[:, cut]

    def own_rows(e):
        return (0, 0, 1, 1)[e], pl.ds((0, 1, 0, 1)[e] * ROWS, ROWS)

    copies_kv = {}
    for d in (1, 3, 2):
        h = lax.rem(x + d, X)
        e = X - d
        half, rows = own_rows(e)
        dst = kv.at[0, half, core, rows]
        copies_kv[e] = send(kv_send.at[h], dst, s_akv.at[d], r_akv.at[d], along_x[d])
    qs[0, :ROWS] = q_send[x]
    kv[0, 0, core, :ROWS] = kv_send[x]

    def rows_of(p):
        return pl.ds(pl.multiple_of(lax.rem(p, 2) * ROWS, ROWS), ROWS)

    def ring(r, p, src):
        dst = kv.at[p // 2 + 1, r, core, rows_of(p)]
        target = along_z[1] if r == 0 else along_z[Z - 1]
        return remote(src, dst, s_ring.at[r, p], r_ring.at[r, p], target)

    def arrived(r, p):
        return kv.at[p // 2 + 1, r, core, rows_of(p)]

    def across(r, p):
        here = arrived(r, p)
        return remote(here, here, s_twin.at[r, p], r_twin.at[r, p], twin)

    def across_own(r):
        here = kv.at[0, r, core]
        return remote(here, here, s_own.at[r], r_own.at[r], twin)

    order = ((0, 1, 3, 2), (0, 3, 2, 1))

    def ring_own(r, p):
        half, rows = own_rows(order[r][p])
        ring(r, p, kv.at[0, half, core, rows]).start()

    for r in range(2):
        ring_own(r, 0)
    top[...] = jnp.full_like(top, -1e30)
    for ref in (acc1, acc2, total, slope):
        ref[...] = jnp.zeros_like(ref)
    for copy in copies_q:
        copy.wait_recv()
    copies_q = [
        send(qs.at[0], qs.at[Y - d], s_yq.at[d], r_yq.at[d], along_y[d]) for d in (2, 1, 3)
    ]
    for e in (1, 3):
        copies_kv[e].wait_recv()
    ring_own(0, 1)
    ring_own(1, 1)
    ring_own(0, 2)
    across_own(0).start()
    copies_kv[2].wait_recv()
    ring_own(1, 2)
    ring_own(0, 3)
    ring_own(1, 3)
    across_own(1).start()

    for copy in copies_w:
        copy.wait_recv()
    own_y = pl.ds(y * 2, 2)
    half_a, half_b = pl.ds(0, 256), pl.ds(256, 256)
    copies_a1, copies_b1 = [], []
    for d in (1, 3, 2):
        here = wbuf.at[x, own_y, core, :, half_a]
        copies_a1.append(send(here, here, s_w1.at[0, d], r_w1.at[0, d], along_y[d]))
        here = wbuf.at[x, own_y, core, :, half_b]
        copies_b1.append(send(here, here, s_w1.at[1, d], r_w1.at[1, d], along_x[d]))

    def poll(p):
        for r in range(2):
            ring(r, p, arrived(r, p)).wait_recv()
            across(r, p).start()

        @pl.when(p <= 9)
        def _():
            ring(0, p + 4, arrived(0, p)).start()

        @pl.when(p <= 7)
        def _():
            ring(1, p + 4, arrived(1, p)).start()

        @pl.when((p == 9) | (p == 10))
        def _():
            ring(1, p + 3, arrived(1, p)).start()

    def take(slot):
        for p in (slot * 2 - 2, slot * 2 - 1):
            for r in range(2):
                across(r, p).wait_recv()

    qs_rows = qs.reshape(Y * BLOCK, 256)
    poll(0)
    poll(1)
    for copy in copies_q:
        copy.wait_recv()

    def weight_rows(d):
        rows_y = pl.ds(lax.rem(y + d, Y) * 2, 2)
        return (
            wbuf.at[lax.rem(x + d, X), :, core, :, half_a],
            wbuf.at[:, rows_y, core, :, half_b],
        )

    def cross(i, d):
        here = weight_rows(d)[i]
        return remote(here, here, s_w3.at[i, d], r_w3.at[i, d], twin)

    def second(i, d):
        here = weight_rows(0)[i]
        target = (along_x, along_y)[i][d]
        return remote(here, here, s_w2.at[i, d], r_w2.at[i, d], target)

    def steps_w(h):
        @pl.when(h == 1)
        def _():
            for copy in copies_b1:
                copy.wait_recv()
            for d in (1, 3, 2):
                second(1, d).start()

        @pl.when(h == 3)
        def _():
            for copy in copies_a1:
                copy.wait_recv()
            for d in (1, 3, 2):
                second(0, d).start()

    for r in range(2):
        across_own(r).wait_recv()

    def body(h, carry):
        @pl.when((h != 5) & (h != 9) & (h != 13))
        def _():
            poll(h + 2 - jnp.where(h > 5, 1, 0) - jnp.where(h > 9, 1, 0))

        slot = h // 2

        @pl.when((h >= 2) & (lax.rem(h, 2) == 0))
        def _():
            take(slot)

        rows = pl.ds(pl.multiple_of(lax.rem(h, 2) * 512, 512), 512)
        fold(kv[slot].reshape(512, 512), qs_rows, acc1, acc2, top, total, slope, rows)
        steps_w(h)
        return carry

    lax.fori_loop(0, PIECES, body, 0)

    poll(PIECES - 1)
    take(PIECES // 2)
    lane = lax.broadcasted_iota(jnp.int32, (BLOCK, 128), 1)

    def part_copy(d, g):
        rows = pl.ds(g * ROWS, ROWS)
        target = device(x, lax.rem(y + d, Y), z, core)
        return remote(
            part_send.at[d, rows], part.at[Y - d, rows], s_part.at[d, g], r_part.at[d, g], target
        )

    def stat_copy(d):
        target = device(x, lax.rem(y + d, Y), z, core)
        return remote(stat_send.at[d], stat.at[Y - d], s_stat.at[d], r_stat.at[d], target)

    def last(i, carry):
        d = lax.rem(i * 3 + 2, Y)
        d = jnp.where(i == 2, 3, jnp.where(i == 3, 0, d))
        rows = pl.ds(pl.multiple_of(d * BLOCK, BLOCK), BLOCK)
        fold(kv[PIECES // 2].reshape(512, 512), qs_rows, acc1, acc2, top, total, slope, rows)
        both = acc1[rows, :]
        acc1[rows, 128:] = both[:, 128:] + acc2[rows, :] * SCALE
        part_send[d, :, :128] = both[:, :128].astype(jnp.bfloat16)
        part_send[d, :, 128:] = acc1[rows, 128:].astype(jnp.bfloat16)
        all_total = jnp.sum(total[rows, :], axis=1, keepdims=True)
        all_slope = jnp.sum(slope[rows, :], axis=1, keepdims=True) * SCALE
        packed = jnp.where(lane == 0, top[rows, :], jnp.where(lane == 1, all_total, all_slope))
        stat_send[d] = packed.T[:8]

        @pl.when(i < 3)
        def _():
            stat_copy(d).start()
            for g in (2, 1, 3, 0):
                part_copy(d, g).start()

        return carry

    lax.fori_loop(0, Y, last, 0)
    for i in range(2):
        cross(i, 0).start()
    for i, d in ((1, 1), (1, 3), (0, 1), (0, 3), (1, 2), (0, 2)):
        second(i, X - d).wait_recv()
        cross(i, d).start()
    out_copies = [pltpu.make_async_copy(wbuf.at[:, :, core], wout_hbm.at[:, :, core], s_out.at[0])]
    out_copies[0].start()

    for d in (2, 1, 3):
        stat_copy(d).wait_recv()
    stats = [stat_send[0]] + [stat[e] for e in range(1, Y)]
    highest = functools.reduce(jnp.maximum, [a[0:1] for a in stats])
    gains = [jnp.exp2(a[0:1] - highest) for a in stats]
    inverse = 1.0 / functools.reduce(jnp.add, [a[1:2] * b for a, b in zip(stats, gains)])
    tilt = functools.reduce(jnp.add, [a[2:3] * b for a, b in zip(stats, gains)]) * inverse
    factors = jnp.concatenate([b * inverse for b in gains] + [tilt], axis=0)
    factors = jnp.concatenate([factors, jnp.zeros((123, BLOCK), jnp.float32)], axis=0).T

    copies_ret = []
    for g in (2, 1, 3, 0):
        rows = slice(g * ROWS, (g + 1) * ROWS)
        gain = [jnp.broadcast_to(factors[rows, e : e + 1], (ROWS, 128)) for e in range(Y + 1)]
        mixed, dmixed = acc1[rows, :128] * gain[0], acc1[rows, 128:] * gain[0]
        for e in (2, 1, 3):
            part_copy(Y - e, g).wait_recv()
            mixed = mixed + part[e, rows, :128].astype(jnp.float32) * gain[e]
            dmixed = dmixed + part[e, rows, 128:].astype(jnp.float32) * gain[e]
        dmixed = dmixed - gain[Y] * mixed
        mix[g, 0] = mixed.astype(jnp.bfloat16)
        mix[g, 1] = dmixed.astype(jnp.bfloat16)
        if g:
            copies_ret.append(
                send(mix.at[g], heads_hbm.at[x], s_ret.at[g], r_ret.at[g], along_x[g])
            )
    out_copies.append(pltpu.make_async_copy(mix.at[0], heads_hbm.at[x], s_out.at[1]))
    out_copies[1].start()
    for i in range(2):
        for d in range(Y):
            cross(i, d).wait_recv()
    there = 1 - core
    out_copies.append(
        pltpu.make_async_copy(wbuf.at[:, :, there], wout_hbm.at[:, :, there], s_out.at[2])
    )
    out_copies[2].start()
    for copy in copies_ret:
        copy.wait_recv()
    for copy in out_copies:
        copy.wait()

    for copy in sends:
        copy.wait_send()
    for d in range(Y):
        for i in range(2):
            cross(i, d).wait_send()
        if d:
            for i in range(2):
                second(i, d).wait_send()
            stat_copy(d).wait_send()
            for g in range(X):
                part_copy(d, g).wait_send()
    for r in range(2):
        across_own(r).wait_send()
        for p in range(PIECES):
            ring(r, p, arrived(r, p)).wait_send()
            across(r, p).wait_send()


def project(heads_hbm, weight_hbm, out_hbm, tout_hbm, heads, weight, result, s_in, s_out):
    first = pltpu.make_async_copy(heads_hbm, heads, s_in.at[X])
    first.start()
    loads = [pltpu.make_async_copy(weight_hbm.at[i], weight.at[i], s_in.at[i]) for i in range(X)]
    for copy in loads:
        copy.start()
    first.wait()
    lhs = jnp.concatenate([heads[h].reshape(2 * ROWS, 128) for h in range(X)], axis=1)
    copies = []
    for i in range(X):
        loads[i].wait()
        result[i] = dot(lhs, weight[i].reshape(1280, 512), NT).astype(jnp.bfloat16)
        for k, out in enumerate((out_hbm, tout_hbm)):
            copy = pltpu.make_async_copy(
                result.at[i, pl.ds(k * ROWS, ROWS)], out.at[:, pl.ds(i * 1280, 1280)], s_out.at[i, k]
            )
            copy.start()
            copies.append(copy)
    for copy in copies:
        copy.wait()


def local(*args):
    args = (*args[:-1], args[-1].T)
    bf, f32, vmem, dma = jnp.bfloat16, jnp.float32, pltpu.VMEM, pltpu.SemaphoreType.DMA
    pairs = [
        (X,), (X,), (2, PIECES), (2, PIECES), (2,), (Y,), (Z,), (2, X), (2, X), (2, X), (Y, X), (Y,), (X,),
    ]
    heads, weight = pl.pallas_call(
        kernel,
        out_shape=[
            jax.ShapeDtypeStruct((X, 2, ROWS, 128), bf),
            jax.ShapeDtypeStruct((X, 2 * Y, 2, 80, 512), bf),
        ],
        in_specs=[pl.BlockSpec(memory_space=pltpu.HBM)] * 8,
        out_specs=[pl.BlockSpec(memory_space=pltpu.HBM)] * 2,
        scratch_shapes=[vmem((ROWS, 512), bf)] * 6
        + [
            vmem((3, ROWS), jnp.int32),
            vmem((X, ROWS, 512), bf),
            vmem((X, ROWS, 256), bf),
            vmem((PIECES // 2 + 1, 2, 2, BLOCK // 2, 512), bf),
            vmem((Y, BLOCK, 256), bf),
            vmem((X, 2 * Y, 2, 80, 512), bf),
            vmem((Y * BLOCK, 256), f32),
            vmem((Y * BLOCK, 128), f32),
            vmem((Y * BLOCK, 128), f32),
            vmem((Y * BLOCK, 128), f32),
            vmem((Y * BLOCK, 128), f32),
            vmem((Y, BLOCK, 256), bf),
            vmem((Y, 8, BLOCK), f32),
            vmem((Y, BLOCK, 256), bf),
            vmem((Y, 8, BLOCK), f32),
            vmem((X, 2, ROWS, 128), bf),
        ]
        + [dma((8,)), dma((3,))]
        + [dma(shape) for shape in pairs for _ in range(2)],
        compiler_params=pltpu.CompilerParams(
            collective_id=0, has_side_effects=True, vmem_limit_bytes=58 << 20
        ),
        name="attend",
    )(*args)
    return pl.pallas_call(
        project,
        out_shape=[jax.ShapeDtypeStruct((ROWS, 5120), bf)] * 2,
        in_specs=[pl.BlockSpec(memory_space=pltpu.HBM)] * 2,
        out_specs=[pl.BlockSpec(memory_space=pltpu.HBM)] * 2,
        scratch_shapes=[
            vmem((X, 2, ROWS, 128), bf),
            vmem((X, 2 * Y, 2, 80, 512), bf),
            vmem((X, 2 * ROWS, 1280), bf),
            dma((X + 1,)),
            dma((X, 2)),
        ],
        compiler_params=pltpu.CompilerParams(vmem_limit_bytes=58 << 20),
        name="project",
    )(heads, weight)


def solution(mesh):
    return jax.shard_map(
        local,
        mesh=mesh,
        in_specs=(
            P(("blk", "uly"), None),
            P(("blk", "uly"), None),
            P(("blk", "uly"), None),
            P(("blk", "uly"), None),
            P(("blk", "uly"), None),
            P(("blk", "uly"), None),
            P(None, ("blk", "uly")),
            P("uly", "blk"),
        ),
        out_specs=(P(("blk", "uly"), None), P(("blk", "uly"), None)),
        check_vma=False,
    )
```

```python
import functools

import jax
import jax.numpy as jnp
from jax import lax
from jax.experimental import pallas as pl
from jax.experimental.pallas import tpu as pltpu
from jax.sharding import PartitionSpec as P

MESH = pl.DeviceIdType.MESH
SCALE = 0.08838834764831845
SCALE2 = SCALE * 1.4426950408889634
NT = (((1,), (1,)), ((), ()))
NN = (((1,), (0,)), ((), ()))

X, Y, Z = 4, 4, 8
ROWS = 64
BLOCK = X * ROWS
CUTS = (1024, 2560, 4096, 5120)
PIECES = 14


def dot(a, b, dims):
    return lax.dot_general(a, b, dims, preferred_element_type=jnp.float32)


def place():
    blk, zlo = lax.axis_index("blk"), lax.axis_index("uly")
    return blk // 16, lax.rem(blk // 4, 4), lax.rem(blk // 2, 2) * 4 + zlo, lax.rem(blk, 2)


def device(x, y, z, core):
    return (((x * 4 + y) * 2 + z // 4) * 2 + core, lax.rem(z, 4))


def rotary_tables(pos_ref):
    pair = lax.broadcasted_iota(jnp.int32, (64, 128), 0)
    begin = jnp.where(pair >= 43, 43, jnp.where(pair >= 22, 22, 0))
    length = jnp.where(pair >= 22, 21.0, 22.0)
    frequency = jnp.exp((pair - begin).astype(jnp.float32) / length * -9.210340371976184)
    pos = pos_ref[...].astype(jnp.float32)
    pos = jnp.concatenate([pos, pos], axis=1)
    chosen = jnp.where(pair < 22, pos[0:1], jnp.where(pair < 43, pos[1:2], pos[2:3]))
    angle = chosen * frequency
    cosine, sine = jnp.cos(angle), jnp.sin(angle)
    cosine = jnp.concatenate([cosine, cosine], axis=0)
    sine = jnp.concatenate([-sine, sine], axis=0)
    return cosine.T[:ROWS], sine.T[:ROWS]


def fold(keys, q_ref, acc1, acc2, top, total, slope, rows):
    q = q_ref[rows, :]
    s = dot(q[:, 128:], keys[:, :128], NT)
    t = dot(q, keys[:, :256], NT)
    lanes = [slice(i * 128, (i + 1) * 128) for i in range(keys.shape[0] // 128)]
    high = functools.reduce(jnp.maximum, [s[:, i] for i in lanes])
    old = top[rows, :]
    new = jnp.maximum(old, jnp.max(high, axis=1, keepdims=True) * SCALE2)
    shrink = jnp.exp2(old - new)
    weights = [jnp.exp2(s[:, i] * SCALE2 - new) for i in lanes]
    tilted = [w * t[:, i] for w, i in zip(weights, lanes)]
    top[rows, :] = new
    total[rows, :] = total[rows, :] * shrink + functools.reduce(jnp.add, weights)
    slope[rows, :] = slope[rows, :] * shrink + functools.reduce(jnp.add, tilted)
    low = jnp.concatenate([w.astype(jnp.bfloat16) for w in weights], axis=1)
    tilted = jnp.concatenate([w.astype(jnp.bfloat16) for w in tilted], axis=1)
    both = jnp.concatenate([shrink, shrink], axis=1)
    acc1[rows, :] = acc1[rows, :] * both + dot(low, keys[:, 256:], NN)
    acc2[rows, :] = acc2[rows, :] * shrink + dot(tilted, keys[:, 256:384], NN)


def kernel(
    q_hbm, k_hbm, v_hbm, tq_hbm, tk_hbm, tv_hbm, pos_hbm, w_hbm, heads_hbm, wout_hbm,
    q_ref, k_ref, v_ref, tq_ref, tk_ref, tv_ref, pos_ref,
    kv_send, q_send, kv, qs, wbuf, acc1, acc2, top, total, slope,
    part_send, stat_send, part, stat, mix,
    s_in, s_out, s_akv, r_akv, s_aq, r_aq, s_ring, r_ring, s_twin, r_twin, s_own, r_own, s_yq, r_yq,
    s_wz, r_wz, s_w1, r_w1, s_w2, r_w2, s_w3, r_w3, s_part, r_part, s_stat, r_stat, s_ret, r_ret,
):
    x, y, z, core = place()
    along_x = [device(lax.rem(x + d, X), y, z, core) for d in range(X)]
    along_y = [device(x, lax.rem(y + d, Y), z, core) for d in range(Y)]
    along_z = [device(x, y, lax.rem(z + d, Z), core) for d in range(Z)]
    twin = device(x, y, z, 1 - core)

    zhi, zlo = z // 4, lax.rem(z, 4)
    own_lanes = pl.ds(pl.multiple_of(zlo * 128, 128), 128)
    own_piece = wbuf.at[x, y * 2 + zhi, core, :, own_lanes]
    inputs = [
        (pos_hbm, pos_ref), (tq_hbm, tq_ref), (q_hbm, q_ref), (k_hbm, k_ref), (tk_hbm, tk_ref),
        (v_hbm, v_ref), (tv_hbm, tv_ref), (w_hbm, own_piece),
    ]
    inputs = [pltpu.make_async_copy(a, b, s_in.at[i]) for i, (a, b) in enumerate(inputs)]
    for copy in inputs:
        copy.start()

    barrier = pltpu.get_barrier_semaphore()
    partners = along_x[1:] + along_y[1:] + along_z[1:] + [twin]
    for partner in partners:
        pl.semaphore_signal(barrier, inc=1, device_id=partner, device_id_type=MESH)

    sends = []

    def remote(src, dst, s, r, target):
        return pltpu.make_async_remote_copy(
            src_ref=src, dst_ref=dst, send_sem=s, recv_sem=r, device_id=target, device_id_type=MESH
        )

    def send(*args):
        copy = remote(*args)
        copy.start()
        sends.append(copy)
        return copy

    inputs[0].wait()
    cosine, sine = rotary_tables(pos_ref)

    def rotated(ref, h):
        a = ref[:, h * 128 : (h + 1) * 128].astype(jnp.float32)
        return (a * cosine + pltpu.roll(a, 64, 1) * sine).astype(jnp.bfloat16)

    inputs[7].wait()
    pl.semaphore_wait(barrier, len(partners))
    copies_w = []
    for d in (4, 3, 5, 2, 6, 1, 7):
        copies_w.append(send(own_piece, own_piece, s_wz.at[d], r_wz.at[d], along_z[d]))
    for copy in inputs[1:3]:
        copy.wait()
    for h in range(X):
        q_send[h, :, :128] = rotated(tq_ref, h)
        q_send[h, :, 128:] = rotated(q_ref, h)
    copies_q = []
    for d in (2, 1, 3):
        h = lax.rem(x + d, X)
        e = X - d
        copies_q.append(
            send(q_send.at[h], qs.at[e, 0], s_aq.at[d], r_aq.at[d], along_x[d])
        )
    for copy in inputs[3:7]:
        copy.wait()
    for h in range(X):
        cut = slice(h * 128, (h + 1) * 128)
        kv_send[h, :, :128] = rotated(k_ref, h)
        kv_send[h, :, 128:256] = rotated(tk_ref, h)
        kv_send[h, :, 256:384] = v_ref[:, cut]
        kv_send[h, :, 384:] = tv_ref[:, cut]

    def own_rows(e):
        return (0, 0, 1, 1)[e], pl.ds((0, 1, 0, 1)[e] * ROWS, ROWS)

    copies_kv = {}
    for d in (1, 3, 2):
        h = lax.rem(x + d, X)
        e = X - d
        half, rows = own_rows(e)
        dst = kv.at[0, half, core, rows]
        copies_kv[e] = send(kv_send.at[h], dst, s_akv.at[d], r_akv.at[d], along_x[d])
    qs[0, 0] = q_send[x]
    kv[0, 0, core, :ROWS] = kv_send[x]

    def rows_of(p):
        return pl.ds(pl.multiple_of(lax.rem(p, 2) * ROWS, ROWS), ROWS)

    def ring(r, p, src):
        dst = kv.at[p // 2 + 1, r, core, rows_of(p)]
        target = along_z[1] if r == 0 else along_z[Z - 1]
        return remote(src, dst, s_ring.at[r, p], r_ring.at[r, p], target)

    def arrived(r, p):
        return kv.at[p // 2 + 1, r, core, rows_of(p)]

    def across(r, p):
        here = arrived(r, p)
        return remote(here, here, s_twin.at[r, p], r_twin.at[r, p], twin)

    def across_own(r):
        here = kv.at[0, r, core]
        return remote(here, here, s_own.at[r], r_own.at[r], twin)

    order = ((0, 1, 3, 2), (0, 3, 2, 1))

    def ring_own(r, p):
        half, rows = own_rows(order[r][p])
        ring(r, p, kv.at[0, half, core, rows]).start()

    for r in range(2):
        ring_own(r, 0)
    top[...] = jnp.full_like(top, -1e30)
    for ref in (acc1, acc2, total, slope):
        ref[...] = jnp.zeros_like(ref)
    for copy in copies_q:
        copy.wait_recv()
    copies_q = [
        send(qs.at[:, 0], qs.at[:, Y - d], s_yq.at[d], r_yq.at[d], along_y[d]) for d in (2, 1, 3)
    ]
    for e in (1, 3):
        copies_kv[e].wait_recv()
    ring_own(0, 1)
    ring_own(1, 1)
    ring_own(0, 2)
    across_own(0).start()
    copies_kv[2].wait_recv()
    ring_own(1, 2)
    ring_own(0, 3)
    ring_own(1, 3)
    across_own(1).start()

    for copy in copies_w:
        copy.wait_recv()
    own_y = pl.ds(y * 2, 2)
    half_a, half_b = pl.ds(0, 256), pl.ds(256, 256)
    copies_a1, copies_b1 = [], []
    for d in (1, 3, 2):
        here = wbuf.at[x, own_y, core, :, half_a]
        copies_a1.append(send(here, here, s_w1.at[0, d], r_w1.at[0, d], along_y[d]))
        here = wbuf.at[x, own_y, core, :, half_b]
        copies_b1.append(send(here, here, s_w1.at[1, d], r_w1.at[1, d], along_x[d]))

    def poll(p):
        for r in range(2):
            ring(r, p, arrived(r, p)).wait_recv()
            across(r, p).start()

        @pl.when(p <= 9)
        def _():
            ring(0, p + 4, arrived(0, p)).start()

        @pl.when(p <= 7)
        def _():
            ring(1, p + 4, arrived(1, p)).start()

        @pl.when((p == 9) | (p == 10))
        def _():
            ring(1, p + 3, arrived(1, p)).start()

    def take(slot):
        for p in (slot * 2 - 2, slot * 2 - 1):
            for r in range(2):
                across(r, p).wait_recv()

    qs_rows = qs.reshape(Y * BLOCK, 256)
    poll(0)
    poll(1)
    for copy in copies_q:
        copy.wait_recv()

    def rows_in(buffer, d):
        rows_y = pl.ds(lax.rem(y + d, Y) * 2, 2)
        return (
            buffer.at[lax.rem(x + d, X), :, core, :, half_a],
            buffer.at[:, rows_y, core, :, half_b],
        )

    weight_rows = functools.partial(rows_in, wbuf)
    result_rows = functools.partial(rows_in, wout_hbm)

    def cross(i, d):
        here = weight_rows(d)[i]
        return remote(here, result_rows(d)[i], s_w3.at[i, d], r_w3.at[i, d], twin)

    def second(i, d):
        here = weight_rows(0)[i]
        target = (along_x, along_y)[i][d]
        return remote(here, here, s_w2.at[i, d], r_w2.at[i, d], target)

    def steps_w(h):
        @pl.when(h == 1)
        def _():
            for copy in copies_b1:
                copy.wait_recv()
            for d in (1, 3, 2):
                second(1, d).start()

        @pl.when(h == 3)
        def _():
            for copy in copies_a1:
                copy.wait_recv()
            for d in (1, 3, 2):
                second(0, d).start()

    for r in range(2):
        across_own(r).wait_recv()

    def body(h, carry):
        @pl.when((h != 5) & (h != 9) & (h != 13))
        def _():
            poll(h + 2 - jnp.where(h > 5, 1, 0) - jnp.where(h > 9, 1, 0))

        slot = h // 2

        @pl.when((h >= 2) & (lax.rem(h, 2) == 0))
        def _():
            take(slot)

        rows = pl.ds(pl.multiple_of(lax.rem(h, 2) * 512, 512), 512)
        fold(kv[slot].reshape(512, 512), qs_rows, acc1, acc2, top, total, slope, rows)
        steps_w(h)
        return carry

    lax.fori_loop(0, PIECES, body, 0)

    poll(PIECES - 1)
    for i in range(2):
        cross(i, 0).start()

    def own_last(i, carry):
        rows = pl.ds(pl.multiple_of(i * 512, 512), 512)
        keys = kv[PIECES // 2, :, core].reshape(256, 512)
        fold(keys, qs_rows, acc1, acc2, top, total, slope, rows)
        return carry

    lax.fori_loop(0, 2, own_last, 0)
    take(PIECES // 2)
    lane = lax.broadcasted_iota(jnp.int32, (BLOCK, 128), 1)

    def part_copy(g, d):
        src = part_send.at[g, pl.ds(d * ROWS, ROWS)]
        return remote(src, part.at[g, Y - d], s_part.at[g, d], r_part.at[g, d], along_y[d])

    def stat_copy(g, d):
        src, dst = stat_send.at[g, d], stat.at[g, Y - d]
        return remote(src, dst, s_stat.at[g, d], r_stat.at[g, d], along_y[d])

    def last(i, carry):
        g = jnp.where(i == 2, 3, jnp.where(i == 3, 0, 2 - i))
        rows = pl.ds(pl.multiple_of(g * BLOCK, BLOCK), BLOCK)
        fold(kv[PIECES // 2, :, 1 - core].reshape(256, 512), qs_rows, acc1, acc2, top, total, slope, rows)
        both = acc1[rows, :]
        acc1[rows, 128:] = both[:, 128:] + acc2[rows, :] * SCALE
        part_send[g, :, :128] = both[:, :128].astype(jnp.bfloat16)
        part_send[g, :, 128:] = acc1[rows, 128:].astype(jnp.bfloat16)
        all_total = jnp.sum(total[rows, :], axis=1, keepdims=True)
        all_slope = jnp.sum(slope[rows, :], axis=1, keepdims=True) * SCALE
        packed = jnp.where(lane == 0, top[rows, :], jnp.where(lane == 1, all_total, all_slope))
        packed = packed.T[:8]
        for d in range(Y):
            half = packed[:, d // 2 * 128 : d // 2 * 128 + 128]
            stat_send[g, d] = half if d % 2 == 0 else pltpu.roll(half, ROWS, 1)
        for d in (2, 1, 3):
            stat_copy(g, d).start()
            part_copy(g, d).start()
        return carry

    lax.fori_loop(0, Y, last, 0)
    for i, d in ((1, 1), (1, 3), (0, 1), (0, 3), (1, 2), (0, 2)):
        second(i, X - d).wait_recv()
        cross(i, d).start()
    out_copies = [pltpu.make_async_copy(wbuf.at[:, :, core], wout_hbm.at[:, :, core], s_out.at[0])]
    out_copies[0].start()

    copies_ret = []
    for g in (2, 1, 3, 0):
        for d in (2, 1, 3):
            stat_copy(g, d).wait_recv()
        stats = [stat_send[g, 0]] + [stat[g, e] for e in range(1, Y)]
        highest = functools.reduce(jnp.maximum, [a[0:1] for a in stats])
        gains = [jnp.exp2(a[0:1] - highest) for a in stats]
        inverse = 1.0 / functools.reduce(jnp.add, [a[1:2] * b for a, b in zip(stats, gains)])
        tilt = functools.reduce(jnp.add, [a[2:3] * b for a, b in zip(stats, gains)]) * inverse
        factors = [b * inverse for b in gains] + [tilt, jnp.zeros((127 - Y, 128), jnp.float32)]
        factors = jnp.concatenate(factors, axis=0).T[:ROWS]
        gain = [jnp.broadcast_to(factors[:, e : e + 1], (ROWS, 128)) for e in range(Y + 1)]
        rows = slice(g * BLOCK, g * BLOCK + ROWS)
        mixed, dmixed = acc1[rows, :128] * gain[0], acc1[rows, 128:] * gain[0]
        for e in (2, 1, 3):
            part_copy(g, Y - e).wait_recv()
            mixed = mixed + part[g, e, :, :128].astype(jnp.float32) * gain[e]
            dmixed = dmixed + part[g, e, :, 128:].astype(jnp.float32) * gain[e]
        dmixed = dmixed - gain[Y] * mixed
        mix[g, 0] = mixed.astype(jnp.bfloat16)
        mix[g, 1] = dmixed.astype(jnp.bfloat16)
        if g:
            copies_ret.append(
                send(mix.at[g], heads_hbm.at[x], s_ret.at[g], r_ret.at[g], along_x[g])
            )
    out_copies.append(pltpu.make_async_copy(mix.at[0], heads_hbm.at[x], s_out.at[1]))
    out_copies[1].start()
    for i in range(2):
        for d in range(Y):
            cross(i, d).wait_recv()
    for copy in copies_ret:
        copy.wait_recv()
    for copy in out_copies:
        copy.wait()

    for copy in sends:
        copy.wait_send()
    for d in range(Y):
        for i in range(2):
            cross(i, d).wait_send()
        if d:
            for i in range(2):
                second(i, d).wait_send()
            for g in range(X):
                stat_copy(g, d).wait_send()
                part_copy(g, d).wait_send()
    for r in range(2):
        across_own(r).wait_send()
        for p in range(PIECES):
            ring(r, p, arrived(r, p)).wait_send()
            across(r, p).wait_send()


def project(heads_hbm, weight_hbm, out_hbm, tout_hbm, heads, weight, result, s_in, s_out):
    first = pltpu.make_async_copy(heads_hbm, heads, s_in.at[len(CUTS)])
    first.start()
    loads = []
    done = 0
    for i, end in enumerate(CUTS):
        units = pl.ds(done, -(-end // 160) - done)
        loads.append(pltpu.make_async_copy(weight_hbm.at[units], weight.at[units], s_in.at[i]))
        loads[i].start()
        done = -(-end // 160)
    first.wait()
    lhs = jnp.concatenate([heads[h].reshape(2 * ROWS, 128) for h in range(X)], axis=1)
    columns = weight.reshape(5120, 512)
    copies = []
    begin = 0
    for i, end in enumerate(CUTS):
        loads[i].wait()
        result[:, begin:end] = dot(lhs, columns[begin:end, :], NT).astype(jnp.bfloat16)
        for k, out in enumerate((out_hbm, tout_hbm)):
            cut = pl.ds(begin, end - begin)
            copies.append(
                pltpu.make_async_copy(
                    result.at[pl.ds(k * ROWS, ROWS), cut], out.at[:, cut], s_out.at[i, k]
                )
            )
            copies[-1].start()
        begin = end
    for copy in copies:
        copy.wait()


def local(*args):
    args = (*args[:-1], args[-1].T)
    bf, f32, vmem, dma = jnp.bfloat16, jnp.float32, pltpu.VMEM, pltpu.SemaphoreType.DMA
    pairs = [
        (X,), (X,), (2, PIECES), (2, PIECES), (2,), (Y,), (Z,), (2, X), (2, X), (2, X), (X, Y), (X, Y), (X,),
    ]
    heads, weight = pl.pallas_call(
        kernel,
        out_shape=[
            jax.ShapeDtypeStruct((X, 2, ROWS, 128), bf),
            jax.ShapeDtypeStruct((X, 2 * Y, 2, 80, 512), bf),
        ],
        in_specs=[pl.BlockSpec(memory_space=pltpu.HBM)] * 8,
        out_specs=[pl.BlockSpec(memory_space=pltpu.HBM)] * 2,
        scratch_shapes=[vmem((ROWS, 512), bf)] * 6
        + [
            vmem((3, ROWS), jnp.int32),
            vmem((X, ROWS, 512), bf),
            vmem((X, ROWS, 256), bf),
            vmem((PIECES // 2 + 1, 2, 2, BLOCK // 2, 512), bf),
            vmem((X, Y, ROWS, 256), bf),
            vmem((X, 2 * Y, 2, 80, 512), bf),
            vmem((Y * BLOCK, 256), f32),
            vmem((Y * BLOCK, 128), f32),
            vmem((Y * BLOCK, 128), f32),
            vmem((Y * BLOCK, 128), f32),
            vmem((Y * BLOCK, 128), f32),
            vmem((X, BLOCK, 256), bf),
            vmem((X, Y, 8, 128), f32),
            vmem((X, Y, ROWS, 256), bf),
            vmem((X, Y, 8, 128), f32),
            vmem((X, 2, ROWS, 128), bf),
        ]
        + [dma((8,)), dma((3,))]
        + [dma(shape) for shape in pairs for _ in range(2)],
        compiler_params=pltpu.CompilerParams(
            collective_id=0, has_side_effects=True, vmem_limit_bytes=58 << 20
        ),
        name="attend",
    )(*args)
    return pl.pallas_call(
        project,
        out_shape=[jax.ShapeDtypeStruct((ROWS, 5120), bf)] * 2,
        in_specs=[pl.BlockSpec(memory_space=pltpu.HBM)] * 2,
        out_specs=[pl.BlockSpec(memory_space=pltpu.HBM)] * 2,
        scratch_shapes=[
            vmem((X, 2, ROWS, 128), bf),
            vmem((4 * Y * 2, 160, 512), bf),
            vmem((2 * ROWS, 5120), bf),
            dma((len(CUTS) + 1,)),
            dma((len(CUTS), 2)),
        ],
        compiler_params=pltpu.CompilerParams(vmem_limit_bytes=58 << 20),
        name="project",
    )(heads, weight.reshape(4 * Y * 2, 160, 512))


def solution(mesh):
    return jax.shard_map(
        local,
        mesh=mesh,
        in_specs=(
            P(("blk", "uly"), None),
            P(("blk", "uly"), None),
            P(("blk", "uly"), None),
            P(("blk", "uly"), None),
            P(("blk", "uly"), None),
            P(("blk", "uly"), None),
            P(None, ("blk", "uly")),
            P("uly", "blk"),
        ),
        out_specs=(P(("blk", "uly"), None), P(("blk", "uly"), None)),
        check_vma=False,
    )
```

```python
import functools

import jax
import jax.numpy as jnp
from jax import lax
from jax.experimental import pallas as pl
from jax.experimental.pallas import tpu as pltpu
from jax.sharding import PartitionSpec as P

MESH = pl.DeviceIdType.MESH
SCALE = 0.08838834764831845
SCALE2 = SCALE * 1.4426950408889634
NT = (((1,), (1,)), ((), ()))
NN = (((1,), (0,)), ((), ()))

X, Y, Z = 4, 4, 8
ROWS = 64
BLOCK = X * ROWS
CUTS = (1024, 2560, 4096, 5120)
PIECES = 14


def dot(a, b, dims):
    return lax.dot_general(a, b, dims, preferred_element_type=jnp.float32)


def place():
    blk, zlo = lax.axis_index("blk"), lax.axis_index("uly")
    return blk // 16, lax.rem(blk // 4, 4), lax.rem(blk // 2, 2) * 4 + zlo, lax.rem(blk, 2)


def device(x, y, z, core):
    return (((x * 4 + y) * 2 + z // 4) * 2 + core, lax.rem(z, 4))


def rotary_tables(pos_ref):
    pair = lax.broadcasted_iota(jnp.int32, (64, 128), 0)
    begin = jnp.where(pair >= 43, 43, jnp.where(pair >= 22, 22, 0))
    length = jnp.where(pair >= 22, 21.0, 22.0)
    frequency = jnp.exp((pair - begin).astype(jnp.float32) / length * -9.210340371976184)
    pos = pos_ref[...].astype(jnp.float32)
    pos = jnp.concatenate([pos, pos], axis=1)
    chosen = jnp.where(pair < 22, pos[0:1], jnp.where(pair < 43, pos[1:2], pos[2:3]))
    angle = chosen * frequency
    cosine, sine = jnp.cos(angle), jnp.sin(angle)
    cosine = jnp.concatenate([cosine, cosine], axis=0)
    sine = jnp.concatenate([-sine, sine], axis=0)
    return cosine.T[:ROWS], sine.T[:ROWS]


def fold(keys, q_ref, acc1, acc2, top, total, slope, rows):
    q = q_ref[rows, :]
    s = dot(q[:, 128:], keys[:, :128], NT)
    t = dot(q, keys[:, :256], NT)
    lanes = [slice(i * 128, (i + 1) * 128) for i in range(keys.shape[0] // 128)]
    high = functools.reduce(jnp.maximum, [s[:, i] for i in lanes])
    old = top[rows, :]
    new = jnp.maximum(old, jnp.max(high, axis=1, keepdims=True) * SCALE2)
    shrink = jnp.exp2(old - new)
    weights = [jnp.exp2(s[:, i] * SCALE2 - new) for i in lanes]
    tilted = [w * t[:, i] for w, i in zip(weights, lanes)]
    top[rows, :] = new
    total[rows, :] = total[rows, :] * shrink + functools.reduce(jnp.add, weights)
    slope[rows, :] = slope[rows, :] * shrink + functools.reduce(jnp.add, tilted)
    low = jnp.concatenate([w.astype(jnp.bfloat16) for w in weights], axis=1)
    tilted = jnp.concatenate([w.astype(jnp.bfloat16) for w in tilted], axis=1)
    both = jnp.concatenate([shrink, shrink], axis=1)
    acc1[rows, :] = acc1[rows, :] * both + dot(low, keys[:, 256:], NN)
    acc2[rows, :] = acc2[rows, :] * shrink + dot(tilted, keys[:, 256:384], NN)


def kernel(
    q_hbm, k_hbm, v_hbm, tq_hbm, tk_hbm, tv_hbm, pos_hbm, w_hbm, heads_hbm, wout_hbm,
    q_ref, k_ref, v_ref, tq_ref, tk_ref, tv_ref, pos_ref,
    kv_send, q_send, kv, qs, wbuf, acc1, acc2, top, total, slope,
    part_send, stat_send, part, stat, mix,
    s_in, s_out, s_akv, r_akv, s_aq, r_aq, s_ring, r_ring, s_twin, r_twin, s_own, r_own, s_yq, r_yq,
    s_wz, r_wz, s_w1, r_w1, s_w2, r_w2, s_w3, r_w3, s_part, r_part, s_stat, r_stat, s_ret, r_ret,
):
    x, y, z, core = place()
    along_x = [device(lax.rem(x + d, X), y, z, core) for d in range(X)]
    along_y = [device(x, lax.rem(y + d, Y), z, core) for d in range(Y)]
    along_z = [device(x, y, lax.rem(z + d, Z), core) for d in range(Z)]
    twin = device(x, y, z, 1 - core)

    zhi, zlo = z // 4, lax.rem(z, 4)
    own_lanes = pl.ds(pl.multiple_of(zlo * 128, 128), 128)
    own_piece = wbuf.at[x, y * 2 + zhi, core, :, own_lanes]
    barrier = pltpu.get_barrier_semaphore()
    partners = along_x[1:] + along_y[1:] + along_z[1:] + [twin]
    for partner in partners:
        pl.semaphore_signal(barrier, inc=1, device_id=partner, device_id_type=MESH)

    inputs = [
        (pos_hbm, pos_ref), (tq_hbm, tq_ref), (q_hbm, q_ref), (k_hbm, k_ref), (tk_hbm, tk_ref),
        (v_hbm, v_ref), (tv_hbm, tv_ref), (w_hbm, own_piece),
    ]
    inputs = [pltpu.make_async_copy(a, b, s_in.at[i]) for i, (a, b) in enumerate(inputs)]
    for copy in inputs:
        copy.start()

    sends = []

    def remote(src, dst, s, r, target):
        return pltpu.make_async_remote_copy(
            src_ref=src, dst_ref=dst, send_sem=s, recv_sem=r, device_id=target, device_id_type=MESH
        )

    def send(*args):
        copy = remote(*args)
        copy.start()
        sends.append(copy)
        return copy

    inputs[0].wait()
    cosine, sine = rotary_tables(pos_ref)

    def rotated(ref, h):
        a = ref[:, h * 128 : (h + 1) * 128].astype(jnp.float32)
        return (a * cosine + pltpu.roll(a, 64, 1) * sine).astype(jnp.bfloat16)

    inputs[7].wait()
    pl.semaphore_wait(barrier, len(partners))
    copies_w = []
    for d in (4, 3, 5, 2, 6, 1, 7):
        copies_w.append(send(own_piece, own_piece, s_wz.at[d], r_wz.at[d], along_z[d]))
    for copy in inputs[1:3]:
        copy.wait()
    for h in range(X):
        q_send[h, :, :128] = rotated(tq_ref, h)
        q_send[h, :, 128:] = rotated(q_ref, h)
    copies_q = []
    for d in (2, 1, 3):
        h = lax.rem(x + d, X)
        e = X - d
        copies_q.append(
            send(q_send.at[h], qs.at[e, 0], s_aq.at[d], r_aq.at[d], along_x[d])
        )
    for copy in inputs[3:7]:
        copy.wait()
    for h in range(X):
        cut = slice(h * 128, (h + 1) * 128)
        kv_send[h, :, :128] = rotated(k_ref, h)
        kv_send[h, :, 128:256] = rotated(tk_ref, h)
        kv_send[h, :, 256:384] = v_ref[:, cut]
        kv_send[h, :, 384:] = tv_ref[:, cut]

    def own_rows(e):
        return (0, 0, 1, 1)[e], pl.ds((0, 1, 0, 1)[e] * ROWS, ROWS)

    copies_kv = {}
    for d in (1, 3, 2):
        h = lax.rem(x + d, X)
        e = X - d
        half, rows = own_rows(e)
        dst = kv.at[0, half, core, rows]
        copies_kv[e] = send(kv_send.at[h], dst, s_akv.at[d], r_akv.at[d], along_x[d])
    qs[0, 0] = q_send[x]
    kv[0, 0, core, :ROWS] = kv_send[x]

    def rows_of(p):
        return pl.ds(pl.multiple_of(lax.rem(p, 2) * ROWS, ROWS), ROWS)

    def ring(r, p, src):
        dst = kv.at[p // 2 + 1, r, core, rows_of(p)]
        target = along_z[1] if r == 0 else along_z[Z - 1]
        return remote(src, dst, s_ring.at[r, p], r_ring.at[r, p], target)

    def arrived(r, p):
        return kv.at[p // 2 + 1, r, core, rows_of(p)]

    def across(r, p):
        here = arrived(r, p)
        return remote(here, here, s_twin.at[r, p], r_twin.at[r, p], twin)

    def across_own(r):
        here = kv.at[0, r, core]
        return remote(here, here, s_own.at[r], r_own.at[r], twin)

    order = ((0, 1, 3, 2), (0, 3, 2, 1))

    def ring_own(r, p):
        half, rows = own_rows(order[r][p])
        ring(r, p, kv.at[0, half, core, rows]).start()

    for r in range(2):
        ring_own(r, 0)
    top[...] = jnp.full_like(top, -1e30)
    for ref in (acc1, acc2, total, slope):
        ref[...] = jnp.zeros_like(ref)
    for copy in copies_q:
        copy.wait_recv()
    copies_q = [
        send(qs.at[:, 0], qs.at[:, Y - d], s_yq.at[d], r_yq.at[d], along_y[d]) for d in (2, 1, 3)
    ]
    for e in (1, 3):
        copies_kv[e].wait_recv()
    ring_own(0, 1)
    ring_own(1, 1)
    ring_own(0, 2)
    across_own(0).start()
    copies_kv[2].wait_recv()
    ring_own(1, 2)
    ring_own(0, 3)
    ring_own(1, 3)
    across_own(1).start()

    for copy in copies_w:
        copy.wait_recv()
    own_y = pl.ds(y * 2, 2)
    half_a, half_b = pl.ds(0, 256), pl.ds(256, 256)
    copies_a1, copies_b1 = [], []
    for d in (1, 3, 2):
        here = wbuf.at[x, own_y, core, :, half_a]
        copies_a1.append(send(here, here, s_w1.at[0, d], r_w1.at[0, d], along_y[d]))
        here = wbuf.at[x, own_y, core, :, half_b]
        copies_b1.append(send(here, here, s_w1.at[1, d], r_w1.at[1, d], along_x[d]))

    def poll(p):
        ring(0, p, arrived(0, p)).wait_recv()

        @pl.when(p <= 9)
        def _():
            ring(0, p + 4, arrived(0, p)).start()

        ring(1, p, arrived(1, p)).wait_recv()

        @pl.when(p <= 7)
        def _():
            ring(1, p + 4, arrived(1, p)).start()

        @pl.when((p == 9) | (p == 10))
        def _():
            ring(1, p + 3, arrived(1, p)).start()

        for r in range(2):
            across(r, p).start()

    def take(slot):
        for p in (slot * 2 - 2, slot * 2 - 1):
            for r in range(2):
                across(r, p).wait_recv()

    qs_rows = qs.reshape(Y * BLOCK, 256)
    poll(0)
    poll(1)
    for copy in copies_q:
        copy.wait_recv()

    def rows_in(buffer, d):
        rows_y = pl.ds(lax.rem(y + d, Y) * 2, 2)
        return (
            buffer.at[lax.rem(x + d, X), :, core, :, half_a],
            buffer.at[:, rows_y, core, :, half_b],
        )

    weight_rows = functools.partial(rows_in, wbuf)
    result_rows = functools.partial(rows_in, wout_hbm)

    def cross(i, d):
        here = weight_rows(d)[i]
        return remote(here, result_rows(d)[i], s_w3.at[i, d], r_w3.at[i, d], twin)

    def second(i, d):
        here = weight_rows(0)[i]
        target = (along_x, along_y)[i][d]
        return remote(here, here, s_w2.at[i, d], r_w2.at[i, d], target)

    def steps_w(h):
        @pl.when(h == 1)
        def _():
            for copy in copies_b1:
                copy.wait_recv()
            for d in (1, 3, 2):
                second(1, d).start()

        @pl.when(h == 3)
        def _():
            for copy in copies_a1:
                copy.wait_recv()
            for d in (1, 3, 2):
                second(0, d).start()

    for r in range(2):
        across_own(r).wait_recv()

    def body(h, carry):
        @pl.when((h != 5) & (h != 9) & (h != 13))
        def _():
            poll(h + 2 - jnp.where(h > 5, 1, 0) - jnp.where(h > 9, 1, 0))

        slot = h // 2

        @pl.when((h >= 2) & (lax.rem(h, 2) == 0))
        def _():
            take(slot)

        rows = pl.ds(pl.multiple_of(lax.rem(h, 2) * 512, 512), 512)
        fold(kv[slot].reshape(512, 512), qs_rows, acc1, acc2, top, total, slope, rows)
        steps_w(h)
        return carry

    lax.fori_loop(0, PIECES, body, 0)

    poll(PIECES - 1)
    for i in range(2):
        cross(i, 0).start()

    def own_last(i, carry):
        rows = pl.ds(pl.multiple_of(i * 512, 512), 512)
        keys = kv[PIECES // 2, :, core].reshape(256, 512)
        fold(keys, qs_rows, acc1, acc2, top, total, slope, rows)
        return carry

    lax.fori_loop(0, 2, own_last, 0)
    take(PIECES // 2)
    lane = lax.broadcasted_iota(jnp.int32, (BLOCK, 128), 1)

    def part_copy(g, d):
        src = part_send.at[g, pl.ds(d * ROWS, ROWS)]
        return remote(src, part.at[g, Y - d], s_part.at[g, d], r_part.at[g, d], along_y[d])

    def stat_copy(g, d):
        src, dst = stat_send.at[g, d], stat.at[g, Y - d]
        return remote(src, dst, s_stat.at[g, d], r_stat.at[g, d], along_y[d])

    def last(i, carry):
        g = jnp.where(i == 2, 3, jnp.where(i == 3, 0, 2 - i))
        rows = pl.ds(pl.multiple_of(g * BLOCK, BLOCK), BLOCK)
        fold(kv[PIECES // 2, :, 1 - core].reshape(256, 512), qs_rows, acc1, acc2, top, total, slope, rows)
        both = acc1[rows, :]
        acc1[rows, 128:] = both[:, 128:] + acc2[rows, :] * SCALE
        part_send[g, :, :128] = both[:, :128].astype(jnp.bfloat16)
        part_send[g, :, 128:] = acc1[rows, 128:].astype(jnp.bfloat16)
        all_total = jnp.sum(total[rows, :], axis=1, keepdims=True)
        all_slope = jnp.sum(slope[rows, :], axis=1, keepdims=True) * SCALE
        packed = jnp.where(lane == 0, top[rows, :], jnp.where(lane == 1, all_total, all_slope))
        packed = packed.T[:8]
        for d in range(Y):
            half = packed[:, d // 2 * 128 : d // 2 * 128 + 128]
            stat_send[g, d] = half if d % 2 == 0 else pltpu.roll(half, ROWS, 1)
        for d in (2, 1, 3):
            stat_copy(g, d).start()
            part_copy(g, d).start()
        return carry

    lax.fori_loop(0, Y, last, 0)
    for i, d in ((1, 1), (1, 3), (0, 1), (0, 3), (1, 2), (0, 2)):
        second(i, X - d).wait_recv()
        cross(i, d).start()
    out_copies = [pltpu.make_async_copy(wbuf.at[:, :, core], wout_hbm.at[:, :, core], s_out.at[0])]
    out_copies[0].start()

    copies_ret = []
    for g in (2, 1, 3, 0):
        for d in (2, 1, 3):
            stat_copy(g, d).wait_recv()
        stats = [stat_send[g, 0]] + [stat[g, e] for e in range(1, Y)]
        highest = functools.reduce(jnp.maximum, [a[0:1] for a in stats])
        gains = [jnp.exp2(a[0:1] - highest) for a in stats]
        inverse = 1.0 / functools.reduce(jnp.add, [a[1:2] * b for a, b in zip(stats, gains)])
        tilt = functools.reduce(jnp.add, [a[2:3] * b for a, b in zip(stats, gains)]) * inverse
        factors = [b * inverse for b in gains] + [tilt, jnp.zeros((127 - Y, 128), jnp.float32)]
        factors = jnp.concatenate(factors, axis=0).T[:ROWS]
        gain = [jnp.broadcast_to(factors[:, e : e + 1], (ROWS, 128)) for e in range(Y + 1)]
        rows = slice(g * BLOCK, g * BLOCK + ROWS)
        mixed, dmixed = acc1[rows, :128] * gain[0], acc1[rows, 128:] * gain[0]
        for e in (2, 1, 3):
            part_copy(g, Y - e).wait_recv()
            mixed = mixed + part[g, e, :, :128].astype(jnp.float32) * gain[e]
            dmixed = dmixed + part[g, e, :, 128:].astype(jnp.float32) * gain[e]
        dmixed = dmixed - gain[Y] * mixed
        mix[g, 0] = mixed.astype(jnp.bfloat16)
        mix[g, 1] = dmixed.astype(jnp.bfloat16)
        if g:
            copies_ret.append(
                send(mix.at[g], heads_hbm.at[x], s_ret.at[g], r_ret.at[g], along_x[g])
            )
    out_copies.append(pltpu.make_async_copy(mix.at[0], heads_hbm.at[x], s_out.at[1]))
    out_copies[1].start()
    for i in range(2):
        for d in range(Y):
            cross(i, d).wait_recv()
    for copy in copies_ret:
        copy.wait_recv()
    for copy in out_copies:
        copy.wait()

    for copy in sends:
        copy.wait_send()
    for d in range(Y):
        for i in range(2):
            cross(i, d).wait_send()
        if d:
            for i in range(2):
                second(i, d).wait_send()
            for g in range(X):
                stat_copy(g, d).wait_send()
                part_copy(g, d).wait_send()
    for r in range(2):
        across_own(r).wait_send()
        for p in range(PIECES):
            ring(r, p, arrived(r, p)).wait_send()
            across(r, p).wait_send()


def project(heads_hbm, weight_hbm, out_hbm, tout_hbm, heads, weight, result, s_in, s_out):
    first = pltpu.make_async_copy(heads_hbm, heads, s_in.at[len(CUTS)])
    first.start()
    loads = []
    done = 0
    for i, end in enumerate(CUTS):
        units = pl.ds(done, -(-end // 160) - done)
        loads.append(pltpu.make_async_copy(weight_hbm.at[units], weight.at[units], s_in.at[i]))
        loads[i].start()
        done = -(-end // 160)
    first.wait()
    lhs = jnp.concatenate([heads[h].reshape(2 * ROWS, 128) for h in range(X)], axis=1)
    columns = weight.reshape(5120, 512)
    copies = []
    begin = 0
    for i, end in enumerate(CUTS):
        loads[i].wait()
        result[:, begin:end] = dot(lhs, columns[begin:end, :], NT).astype(jnp.bfloat16)
        for k, out in enumerate((out_hbm, tout_hbm)):
            cut = pl.ds(begin, end - begin)
            copies.append(
                pltpu.make_async_copy(
                    result.at[pl.ds(k * ROWS, ROWS), cut], out.at[:, cut], s_out.at[i, k]
                )
            )
            copies[-1].start()
        begin = end
    for copy in copies:
        copy.wait()


def local(*args):
    args = (*args[:-1], args[-1].T)
    bf, f32, vmem, dma = jnp.bfloat16, jnp.float32, pltpu.VMEM, pltpu.SemaphoreType.DMA
    pairs = [
        (X,), (X,), (2, PIECES), (2, PIECES), (2,), (Y,), (Z,), (2, X), (2, X), (2, X), (X, Y), (X, Y), (X,),
    ]
    heads, weight = pl.pallas_call(
        kernel,
        out_shape=[
            jax.ShapeDtypeStruct((X, 2, ROWS, 128), bf),
            jax.ShapeDtypeStruct((X, 2 * Y, 2, 80, 512), bf),
        ],
        in_specs=[pl.BlockSpec(memory_space=pltpu.HBM)] * 8,
        out_specs=[pl.BlockSpec(memory_space=pltpu.HBM)] * 2,
        scratch_shapes=[vmem((ROWS, 512), bf)] * 6
        + [
            vmem((3, ROWS), jnp.int32),
            vmem((X, ROWS, 512), bf),
            vmem((X, ROWS, 256), bf),
            vmem((PIECES // 2 + 1, 2, 2, BLOCK // 2, 512), bf),
            vmem((X, Y, ROWS, 256), bf),
            vmem((X, 2 * Y, 2, 80, 512), bf),
            vmem((Y * BLOCK, 256), f32),
            vmem((Y * BLOCK, 128), f32),
            vmem((Y * BLOCK, 128), f32),
            vmem((Y * BLOCK, 128), f32),
            vmem((Y * BLOCK, 128), f32),
            vmem((X, BLOCK, 256), bf),
            vmem((X, Y, 8, 128), f32),
            vmem((X, Y, ROWS, 256), bf),
            vmem((X, Y, 8, 128), f32),
            vmem((X, 2, ROWS, 128), bf),
        ]
        + [dma((8,)), dma((3,))]
        + [dma(shape) for shape in pairs for _ in range(2)],
        compiler_params=pltpu.CompilerParams(
            collective_id=0, has_side_effects=True, vmem_limit_bytes=58 << 20
        ),
        name="attend",
    )(*args)
    return pl.pallas_call(
        project,
        out_shape=[jax.ShapeDtypeStruct((ROWS, 5120), bf)] * 2,
        in_specs=[pl.BlockSpec(memory_space=pltpu.HBM)] * 2,
        out_specs=[pl.BlockSpec(memory_space=pltpu.HBM)] * 2,
        scratch_shapes=[
            vmem((X, 2, ROWS, 128), bf),
            vmem((4 * Y * 2, 160, 512), bf),
            vmem((2 * ROWS, 5120), bf),
            dma((len(CUTS) + 1,)),
            dma((len(CUTS), 2)),
        ],
        compiler_params=pltpu.CompilerParams(vmem_limit_bytes=58 << 20),
        name="project",
    )(heads, weight.reshape(4 * Y * 2, 160, 512))


def solution(mesh):
    return jax.shard_map(
        local,
        mesh=mesh,
        in_specs=(
            P(("blk", "uly"), None),
            P(("blk", "uly"), None),
            P(("blk", "uly"), None),
            P(("blk", "uly"), None),
            P(("blk", "uly"), None),
            P(("blk", "uly"), None),
            P(None, ("blk", "uly")),
            P("uly", "blk"),
        ),
        out_specs=(P(("blk", "uly"), None), P(("blk", "uly"), None)),
        check_vma=False,
    )
```

```python
import functools

import jax
import jax.numpy as jnp
from jax import lax
from jax.experimental import pallas as pl
from jax.experimental.pallas import tpu as pltpu
from jax.sharding import PartitionSpec as P

MESH = pl.DeviceIdType.MESH
SCALE = 0.08838834764831845
SCALE2 = SCALE * 1.4426950408889634
NT = (((1,), (1,)), ((), ()))
NN = (((1,), (0,)), ((), ()))

X, Y, Z = 4, 4, 8
ROWS = 64
BLOCK = X * ROWS
CUTS = (1024, 2560, 4096, 5120)
PIECES = 14


def dot(a, b, dims):
    return lax.dot_general(a, b, dims, preferred_element_type=jnp.float32)


def place():
    blk, zlo = lax.axis_index("blk"), lax.axis_index("uly")
    return blk // 16, lax.rem(blk // 4, 4), lax.rem(blk // 2, 2) * 4 + zlo, lax.rem(blk, 2)


def device(x, y, z, core):
    return (((x * 4 + y) * 2 + z // 4) * 2 + core, lax.rem(z, 4))


def rotary_tables(pos_ref):
    pair = lax.broadcasted_iota(jnp.int32, (64, 128), 0)
    begin = jnp.where(pair >= 43, 43, jnp.where(pair >= 22, 22, 0))
    length = jnp.where(pair >= 22, 21.0, 22.0)
    frequency = jnp.exp((pair - begin).astype(jnp.float32) / length * -9.210340371976184)
    pos = pos_ref[...].astype(jnp.float32)
    pos = jnp.concatenate([pos, pos], axis=1)
    chosen = jnp.where(pair < 22, pos[0:1], jnp.where(pair < 43, pos[1:2], pos[2:3]))
    angle = chosen * frequency
    cosine, sine = jnp.cos(angle), jnp.sin(angle)
    cosine = jnp.concatenate([cosine, cosine], axis=0)
    sine = jnp.concatenate([-sine, sine], axis=0)
    return cosine.T[:ROWS], sine.T[:ROWS]


def fold(keys, q_ref, acc1, acc2, top, total, slope, rows):
    q = q_ref[rows, :]
    s = dot(q[:, 128:], keys[:, :128], NT)
    t = dot(q, keys[:, :256], NT)
    lanes = [slice(i * 128, (i + 1) * 128) for i in range(keys.shape[0] // 128)]
    high = functools.reduce(jnp.maximum, [s[:, i] for i in lanes])
    old = top[rows, :]
    new = jnp.maximum(old, jnp.max(high, axis=1, keepdims=True) * SCALE2)
    shrink = jnp.exp2(old - new)
    weights = [jnp.exp2(s[:, i] * SCALE2 - new) for i in lanes]
    tilted = [w * t[:, i] for w, i in zip(weights, lanes)]
    top[rows, :] = new
    total[rows, :] = total[rows, :] * shrink + functools.reduce(jnp.add, weights)
    slope[rows, :] = slope[rows, :] * shrink + functools.reduce(jnp.add, tilted)
    low = jnp.concatenate([w.astype(jnp.bfloat16) for w in weights], axis=1)
    tilted = jnp.concatenate([w.astype(jnp.bfloat16) for w in tilted], axis=1)
    both = jnp.concatenate([shrink, shrink], axis=1)
    acc1[rows, :] = acc1[rows, :] * both + dot(low, keys[:, 256:], NN)
    acc2[rows, :] = acc2[rows, :] * shrink + dot(tilted, keys[:, 256:384], NN)


def kernel(
    q_hbm, k_hbm, v_hbm, tq_hbm, tk_hbm, tv_hbm, pos_hbm, w_hbm, heads_hbm, wout_hbm,
    q_ref, k_ref, v_ref, tq_ref, tk_ref, tv_ref, pos_ref,
    kv_send, q_send, kv, qs, wbuf, acc1, acc2, top, total, slope,
    part_send, stat_send, part, stat, mix,
    s_in, s_out, s_akv, r_akv, s_aq, r_aq, s_ring, r_ring, s_twin, r_twin, s_own, r_own, s_yq, r_yq,
    s_wz, r_wz, s_w1, r_w1, s_w2, r_w2, s_w3, r_w3, s_part, r_part, s_stat, r_stat, s_ret, r_ret,
):
    x, y, z, core = place()
    along_x = [device(lax.rem(x + d, X), y, z, core) for d in range(X)]
    along_y = [device(x, lax.rem(y + d, Y), z, core) for d in range(Y)]
    along_z = [device(x, y, lax.rem(z + d, Z), core) for d in range(Z)]
    twin = device(x, y, z, 1 - core)

    zhi, zlo = z // 4, lax.rem(z, 4)
    own_lanes = pl.ds(pl.multiple_of(zlo * 128, 128), 128)
    own_piece = wbuf.at[x, y * 2 + zhi, core, :, own_lanes]
    inputs = [
        (pos_hbm, pos_ref), (tq_hbm, tq_ref), (q_hbm, q_ref), (k_hbm, k_ref), (tk_hbm, tk_ref),
        (v_hbm, v_ref), (tv_hbm, tv_ref), (w_hbm, own_piece),
    ]
    inputs = [pltpu.make_async_copy(a, b, s_in.at[i]) for i, (a, b) in enumerate(inputs)]
    for copy in inputs:
        copy.start()

    barrier = pltpu.get_barrier_semaphore()
    partners = along_x[1:] + along_y[1:] + along_z[1:] + [twin]
    for partner in partners:
        pl.semaphore_signal(barrier, inc=1, device_id=partner, device_id_type=MESH)

    sends = []

    def remote(src, dst, s, r, target):
        return pltpu.make_async_remote_copy(
            src_ref=src, dst_ref=dst, send_sem=s, recv_sem=r, device_id=target, device_id_type=MESH
        )

    def send(*args):
        copy = remote(*args)
        copy.start()
        sends.append(copy)
        return copy

    inputs[0].wait()
    cosine, sine = rotary_tables(pos_ref)

    def rotated(ref, h):
        a = ref[:, h * 128 : (h + 1) * 128].astype(jnp.float32)
        return (a * cosine + pltpu.roll(a, 64, 1) * sine).astype(jnp.bfloat16)

    inputs[7].wait()
    pl.semaphore_wait(barrier, len(partners))
    copies_w = []
    for d in (4, 3, 5, 2, 6, 1, 7):
        copies_w.append(send(own_piece, own_piece, s_wz.at[d], r_wz.at[d], along_z[d]))
    for copy in inputs[1:3]:
        copy.wait()
    for h in range(X):
        q_send[h, :, :128] = rotated(tq_ref, h)
        q_send[h, :, 128:] = rotated(q_ref, h)
    copies_q = []
    for d in (2, 1, 3):
        h = lax.rem(x + d, X)
        e = X - d
        copies_q.append(
            send(q_send.at[h], qs.at[e, 0], s_aq.at[d], r_aq.at[d], along_x[d])
        )
    for copy in inputs[3:7]:
        copy.wait()
    for h in range(X):
        cut = slice(h * 128, (h + 1) * 128)
        kv_send[h, :, :128] = rotated(k_ref, h)
        kv_send[h, :, 128:256] = rotated(tk_ref, h)
        kv_send[h, :, 256:384] = v_ref[:, cut]
        kv_send[h, :, 384:] = tv_ref[:, cut]

    def own_rows(e):
        return (0, 0, 1, 1)[e], pl.ds((0, 1, 0, 1)[e] * ROWS, ROWS)

    copies_kv = {}
    for d in (1, 3, 2):
        h = lax.rem(x + d, X)
        e = X - d
        half, rows = own_rows(e)
        dst = kv.at[0, half, core, rows]
        copies_kv[e] = send(kv_send.at[h], dst, s_akv.at[d], r_akv.at[d], along_x[d])
    qs[0, 0] = q_send[x]
    kv[0, 0, core, :ROWS] = kv_send[x]

    def rows_of(p):
        return pl.ds(pl.multiple_of(lax.rem(p, 2) * ROWS, ROWS), ROWS)

    def ring(r, p, src):
        dst = kv.at[p // 2 + 1, r, core, rows_of(p)]
        target = along_z[1] if r == 0 else along_z[Z - 1]
        return remote(src, dst, s_ring.at[r, p], r_ring.at[r, p], target)

    def arrived(r, p):
        return kv.at[p // 2 + 1, r, core, rows_of(p)]

    def across(r, p):
        here = arrived(r, p)
        return remote(here, here, s_twin.at[r, p], r_twin.at[r, p], twin)

    def across_own(r):
        here = kv.at[0, r, core]
        return remote(here, here, s_own.at[r], r_own.at[r], twin)

    order = ((0, 1, 3, 2), (0, 3, 2, 1))

    def ring_own(r, p):
        half, rows = own_rows(order[r][p])
        ring(r, p, kv.at[0, half, core, rows]).start()

    for r in range(2):
        ring_own(r, 0)
    top[...] = jnp.full_like(top, -1e30)
    for ref in (acc1, acc2, total, slope):
        ref[...] = jnp.zeros_like(ref)
    for copy in copies_q:
        copy.wait_recv()
    copies_q = [
        send(qs.at[:, 0], qs.at[:, Y - d], s_yq.at[d], r_yq.at[d], along_y[d]) for d in (2, 1, 3)
    ]
    for e in (1, 3):
        copies_kv[e].wait_recv()
    ring_own(0, 1)
    ring_own(1, 1)
    ring_own(0, 2)
    across_own(0).start()
    copies_kv[2].wait_recv()
    ring_own(1, 2)
    ring_own(0, 3)
    ring_own(1, 3)
    across_own(1).start()

    for copy in copies_w:
        copy.wait_recv()
    own_y = pl.ds(y * 2, 2)
    half_a, half_b = pl.ds(0, 256), pl.ds(256, 256)
    copies_a1, copies_b1 = [], []
    for d in (1, 3, 2):
        here = wbuf.at[x, own_y, core, :, half_a]
        copies_a1.append(send(here, here, s_w1.at[0, d], r_w1.at[0, d], along_y[d]))
        here = wbuf.at[x, own_y, core, :, half_b]
        copies_b1.append(send(here, here, s_w1.at[1, d], r_w1.at[1, d], along_x[d]))

    def poll(p):
        for r in range(2):
            ring(r, p, arrived(r, p)).wait_recv()
            across(r, p).start()

        @pl.when(p <= 9)
        def _():
            ring(0, p + 4, arrived(0, p)).start()

        @pl.when(p <= 7)
        def _():
            ring(1, p + 4, arrived(1, p)).start()

        @pl.when((p == 9) | (p == 10))
        def _():
            ring(1, p + 3, arrived(1, p)).start()

    def take(slot):
        for p in (slot * 2 - 2, slot * 2 - 1):
            for r in range(2):
                across(r, p).wait_recv()

    qs_rows = qs.reshape(Y * BLOCK, 256)
    poll(0)
    poll(1)
    for copy in copies_q:
        copy.wait_recv()

    def rows_in(buffer, d):
        rows_y = pl.ds(lax.rem(y + d, Y) * 2, 2)
        return (
            buffer.at[lax.rem(x + d, X), :, core, :, half_a],
            buffer.at[:, rows_y, core, :, half_b],
        )

    weight_rows = functools.partial(rows_in, wbuf)
    result_rows = functools.partial(rows_in, wout_hbm)

    def cross(i, d):
        here = weight_rows(d)[i]
        return remote(here, result_rows(d)[i], s_w3.at[i, d], r_w3.at[i, d], twin)

    def second(i, d):
        here = weight_rows(0)[i]
        target = (along_x, along_y)[i][d]
        return remote(here, here, s_w2.at[i, d], r_w2.at[i, d], target)

    def steps_w(h):
        @pl.when(h == 1)
        def _():
            for copy in copies_b1:
                copy.wait_recv()
            for d in (1, 3, 2):
                second(1, d).start()

        @pl.when(h == 3)
        def _():
            for copy in copies_a1:
                copy.wait_recv()
            for d in (1, 3, 2):
                second(0, d).start()

    for r in range(2):
        across_own(r).wait_recv()

    def body(h, carry):
        @pl.when((h != 5) & (h != 9) & (h != 13))
        def _():
            poll(h + 2 - jnp.where(h > 5, 1, 0) - jnp.where(h > 9, 1, 0))

        slot = h // 2

        @pl.when((h >= 2) & (lax.rem(h, 2) == 0))
        def _():
            take(slot)

        rows = pl.ds(pl.multiple_of(lax.rem(h, 2) * 512, 512), 512)
        fold(kv[slot].reshape(512, 512), qs_rows, acc1, acc2, top, total, slope, rows)
        steps_w(h)
        return carry

    lax.fori_loop(0, PIECES, body, 0)

    poll(PIECES - 1)
    for i in range(2):
        cross(i, 0).start()

    def own_last(i, carry):
        rows = pl.ds(pl.multiple_of(i * 512, 512), 512)
        keys = kv[PIECES // 2, :, core].reshape(256, 512)
        fold(keys, qs_rows, acc1, acc2, top, total, slope, rows)
        return carry

    lax.fori_loop(0, 2, own_last, 0)
    take(PIECES // 2)
    lane = lax.broadcasted_iota(jnp.int32, (BLOCK, 128), 1)

    def part_copy(g, d):
        src = part_send.at[g, pl.ds(d * ROWS, ROWS)]
        return remote(src, part.at[g, Y - d], s_part.at[g, d], r_part.at[g, d], along_y[d])

    def stat_copy(g, d):
        src, dst = stat_send.at[g, d], stat.at[g, Y - d]
        return remote(src, dst, s_stat.at[g, d], r_stat.at[g, d], along_y[d])

    def last(i, carry):
        g = jnp.where(i == 2, 3, jnp.where(i == 3, 0, 2 - i))
        rows = pl.ds(pl.multiple_of(g * BLOCK, BLOCK), BLOCK)
        fold(kv[PIECES // 2, :, 1 - core].reshape(256, 512), qs_rows, acc1, acc2, top, total, slope, rows)
        both = acc1[rows, :]
        second_sum = both[:, 128:] + acc2[rows, :] * SCALE
        own_rows_of = pl.ds(pl.multiple_of(g * BLOCK, BLOCK), ROWS)
        acc1[own_rows_of, 128:] = second_sum[:ROWS]
        part_send[g, :, :128] = both[:, :128].astype(jnp.bfloat16)
        part_send[g, :, 128:] = second_sum.astype(jnp.bfloat16)
        all_total = jnp.sum(total[rows, :], axis=1, keepdims=True)
        all_slope = jnp.sum(slope[rows, :], axis=1, keepdims=True) * SCALE
        packed = jnp.where(lane == 0, top[rows, :], jnp.where(lane == 1, all_total, all_slope))
        packed = packed.T[:8]
        for d in range(Y):
            half = packed[:, d // 2 * 128 : d // 2 * 128 + 128]
            stat_send[g, d] = half if d % 2 == 0 else pltpu.roll(half, ROWS, 1)
        for d in (2, 1, 3):
            stat_copy(g, d).start()
            part_copy(g, d).start()
        return carry

    lax.fori_loop(0, Y, last, 0)
    for i, d in ((1, 1), (1, 3), (0, 1), (0, 3), (1, 2), (0, 2)):
        second(i, X - d).wait_recv()
        cross(i, d).start()
    out_copies = [pltpu.make_async_copy(wbuf.at[:, :, core], wout_hbm.at[:, :, core], s_out.at[0])]
    out_copies[0].start()

    copies_ret = []
    for g in (2, 1, 3, 0):
        for d in (2, 1, 3):
            stat_copy(g, d).wait_recv()
        stats = [stat_send[g, 0]] + [stat[g, e] for e in range(1, Y)]
        highest = functools.reduce(jnp.maximum, [a[0:1] for a in stats])
        gains = [jnp.exp2(a[0:1] - highest) for a in stats]
        inverse = 1.0 / functools.reduce(jnp.add, [a[1:2] * b for a, b in zip(stats, gains)])
        tilt = functools.reduce(jnp.add, [a[2:3] * b for a, b in zip(stats, gains)]) * inverse
        factors = [b * inverse for b in gains] + [tilt, jnp.zeros((127 - Y, 128), jnp.float32)]
        factors = jnp.concatenate(factors, axis=0).T[:ROWS]
        gain = [jnp.broadcast_to(factors[:, e : e + 1], (ROWS, 128)) for e in range(Y + 1)]
        rows = slice(g * BLOCK, g * BLOCK + ROWS)
        mixed, dmixed = acc1[rows, :128] * gain[0], acc1[rows, 128:] * gain[0]
        for e in (2, 1, 3):
            part_copy(g, Y - e).wait_recv()
            mixed = mixed + part[g, e, :, :128].astype(jnp.float32) * gain[e]
            dmixed = dmixed + part[g, e, :, 128:].astype(jnp.float32) * gain[e]
        dmixed = dmixed - gain[Y] * mixed
        mix[g, 0] = mixed.astype(jnp.bfloat16)
        mix[g, 1] = dmixed.astype(jnp.bfloat16)
        if g:
            copies_ret.append(
                send(mix.at[g], heads_hbm.at[x], s_ret.at[g], r_ret.at[g], along_x[g])
            )
    out_copies.append(pltpu.make_async_copy(mix.at[0], heads_hbm.at[x], s_out.at[1]))
    out_copies[1].start()
    for i in range(2):
        for d in range(Y):
            cross(i, d).wait_recv()
    for copy in copies_ret:
        copy.wait_recv()
    for copy in out_copies:
        copy.wait()

    for copy in sends:
        copy.wait_send()
    for d in range(Y):
        for i in range(2):
            cross(i, d).wait_send()
        if d:
            for i in range(2):
                second(i, d).wait_send()
            for g in range(X):
                stat_copy(g, d).wait_send()
                part_copy(g, d).wait_send()
    for r in range(2):
        across_own(r).wait_send()
        for p in range(PIECES):
            ring(r, p, arrived(r, p)).wait_send()
            across(r, p).wait_send()


def project(heads_hbm, weight_hbm, out_hbm, tout_hbm, heads, weight, result, s_in, s_out):
    first = pltpu.make_async_copy(heads_hbm, heads, s_in.at[len(CUTS)])
    first.start()
    loads = []
    done = 0
    for i, end in enumerate(CUTS):
        units = pl.ds(done, -(-end // 160) - done)
        loads.append(pltpu.make_async_copy(weight_hbm.at[units], weight.at[units], s_in.at[i]))
        loads[i].start()
        done = -(-end // 160)
    first.wait()
    lhs = jnp.concatenate([heads[h].reshape(2 * ROWS, 128) for h in range(X)], axis=1)
    columns = weight.reshape(5120, 512)
    copies = []
    begin = 0
    for i, end in enumerate(CUTS):
        loads[i].wait()
        result[:, begin:end] = dot(lhs, columns[begin:end, :], NT).astype(jnp.bfloat16)
        for k, out in enumerate((out_hbm, tout_hbm)):
            cut = pl.ds(begin, end - begin)
            copies.append(
                pltpu.make_async_copy(
                    result.at[pl.ds(k * ROWS, ROWS), cut], out.at[:, cut], s_out.at[i, k]
                )
            )
            copies[-1].start()
        begin = end
    for copy in copies:
        copy.wait()


def local(*args):
    args = (*args[:-1], args[-1].T)
    bf, f32, vmem, dma = jnp.bfloat16, jnp.float32, pltpu.VMEM, pltpu.SemaphoreType.DMA
    pairs = [
        (X,), (X,), (2, PIECES), (2, PIECES), (2,), (Y,), (Z,), (2, X), (2, X), (2, X), (X, Y), (X, Y), (X,),
    ]
    heads, weight = pl.pallas_call(
        kernel,
        out_shape=[
            jax.ShapeDtypeStruct((X, 2, ROWS, 128), bf),
            jax.ShapeDtypeStruct((X, 2 * Y, 2, 80, 512), bf),
        ],
        in_specs=[pl.BlockSpec(memory_space=pltpu.HBM)] * 8,
        out_specs=[pl.BlockSpec(memory_space=pltpu.HBM)] * 2,
        scratch_shapes=[vmem((ROWS, 512), bf)] * 6
        + [
            vmem((3, ROWS), jnp.int32),
            vmem((X, ROWS, 512), bf),
            vmem((X, ROWS, 256), bf),
            vmem((PIECES // 2 + 1, 2, 2, BLOCK // 2, 512), bf),
            vmem((X, Y, ROWS, 256), bf),
            vmem((X, 2 * Y, 2, 80, 512), bf),
            vmem((Y * BLOCK, 256), f32),
            vmem((Y * BLOCK, 128), f32),
            vmem((Y * BLOCK, 128), f32),
            vmem((Y * BLOCK, 128), f32),
            vmem((Y * BLOCK, 128), f32),
            vmem((X, BLOCK, 256), bf),
            vmem((X, Y, 8, 128), f32),
            vmem((X, Y, ROWS, 256), bf),
            vmem((X, Y, 8, 128), f32),
            vmem((X, 2, ROWS, 128), bf),
        ]
        + [dma((8,)), dma((3,))]
        + [dma(shape) for shape in pairs for _ in range(2)],
        compiler_params=pltpu.CompilerParams(
            collective_id=0, has_side_effects=True, vmem_limit_bytes=58 << 20
        ),
        name="attend",
    )(*args)
    return pl.pallas_call(
        project,
        out_shape=[jax.ShapeDtypeStruct((ROWS, 5120), bf)] * 2,
        in_specs=[pl.BlockSpec(memory_space=pltpu.HBM)] * 2,
        out_specs=[pl.BlockSpec(memory_space=pltpu.HBM)] * 2,
        scratch_shapes=[
            vmem((X, 2, ROWS, 128), bf),
            vmem((4 * Y * 2, 160, 512), bf),
            vmem((2 * ROWS, 5120), bf),
            dma((len(CUTS) + 1,)),
            dma((len(CUTS), 2)),
        ],
        compiler_params=pltpu.CompilerParams(vmem_limit_bytes=58 << 20),
        name="project",
    )(heads, weight.reshape(4 * Y * 2, 160, 512))


def solution(mesh):
    return jax.shard_map(
        local,
        mesh=mesh,
        in_specs=(
            P(("blk", "uly"), None),
            P(("blk", "uly"), None),
            P(("blk", "uly"), None),
            P(("blk", "uly"), None),
            P(("blk", "uly"), None),
            P(("blk", "uly"), None),
            P(None, ("blk", "uly")),
            P("uly", "blk"),
        ),
        out_specs=(P(("blk", "uly"), None), P(("blk", "uly"), None)),
        check_vma=False,
    )
```
